128 devices in a mesh: wide: 32 (over y, z_lo, x), narrow: 4 (over z_hi, core).
Axes of the slice: x: 4, y: 4, z: 4 (z_hi: 2, z_lo: 2; z = z_hi * 2 + z_lo), core: 2. Of those that a mesh axis runs over, the one named last changes fastest.
Arguments:
- token_ids: int32 [2, 256], P(None, 'wide'), may hold values from 0 to 511
- lengths: int32 [256], P(('wide', 'narrow')), may hold values from 1 to 62, as said below
- embedding: bfloat16 [512, 8192], P(None, 'narrow'), may hold values from -6 to 6
- hyena_gain: float32 [8192], P('narrow'), may hold values from 0.1 to 1.9
- hyena_in: bfloat16 [8192, 3, 8192], P('narrow', None, 'wide'), may hold values from -0.0625 to 0.0625
- fir_taps: float32 [3, 3, 8192], P(None, None, 'wide'), may hold values from -3 to 3
- poles: float32 [16, 8192], P(None, 'wide'), may hold values from 0.3 to 0.995
- residues: float32 [16, 8192], P(None, 'wide'), may hold values from -2 to 2
- skip: float32 [8192], P('wide'), may hold values from 0.5 to 1.5
- hyena_out: bfloat16 [8192, 8192], P('wide', 'narrow'), may hold values from -0.0625 to 0.0625
- modal_state: float32 [256, 16, 8192], P('narrow', None, 'wide'), may hold values from -6 to 6
- fir_state: float32 [256, 2, 3, 8192], P('narrow', None, None, 'wide'), may hold values from -6 to 6
- attn_gain: float32 [8192], P('narrow'), may hold values from 0.1 to 1.9
- attn_in: bfloat16 [8192, 3, 8192], P('narrow', None, 'wide'), may hold values from -0.0625 to 0.0625
- attn_out: bfloat16 [8192, 8192], P('wide', 'narrow'), may hold values from -0.0625 to 0.0625
- kv_cache: bfloat16 [256, 64, 2, 8192], P(('wide', 'narrow')), may hold values from -512 to 512
Outputs:
- hidden_states: bfloat16 [2, 256, 8192], P(None, 'wide', 'narrow')
- modal_out: float32 [256, 16, 8192], P('narrow', None, 'wide')
- fir_out: float32 [256, 2, 3, 8192], P('narrow', None, None, 'wide')
The draws below stay inside these ranges and needn't reach their ends.
Inputs may be any that keep to these rules, and one draw needn't show every extreme that they name: `lengths`: a sequence's cache holds valid keys at positions below its length; some sequence has length 62.
All inputs are finite; a program needn't handle non-finite values.
Results may differ from the reference program's by a relative error of at most 0.035.
Values may be sent and summed in bfloat16 or wider, within the bound.
A program may use at most 128 MiB of HBM per device.

```python
import math
import jax
import jax.numpy as jnp
import numpy as np
from jax import lax

D = 8192
HEADS = 64
HEAD_DIM = 128
VOCAB = 512
STATE = 16
TAPS = 3
STEPS = 2
SEQ_DEV = 2
CACHE = 64
SEQS = 256
DEVICES = 128


def draw_lengths(key, part):
    key = jax.random.fold_in(key, 5)
    count = SEQ_DEV * DEVICES
    values = jax.random.randint(key, (count,), 1, CACHE - STEPS + 1)
    chosen = jax.random.randint(jax.random.fold_in(key, 2), (), 0, count)
    return jnp.where(jnp.arange(count) == chosen, CACHE - STEPS, values).astype(jnp.int32)


def draw_kv_cache(key, part):
    key = jax.random.fold_in(key, 11)
    shape = (SEQ_DEV * DEVICES, CACHE, 2, D)
    return jnp.clip(jax.random.normal(key, shape, jnp.float32), -4.0, 4.0).astype(jnp.bfloat16)


def plant(values, stream_key, smallest, high):
    longest = values.shape.index(max(values.shape))
    spots = []
    for shift in (0, 1):
        where = [jax.random.randint(jax.random.fold_in(stream_key, axis), (), 0, length) for axis, length in enumerate(values.shape)]
        where[longest] = (where[longest] + shift) % values.shape[longest]
        spots.append(tuple(where))
    return values.at[spots[0]].set(smallest).at[spots[1]].set(high)


def shard_levels(rng, dims, shards, smallest, largest):
    def one(axis_at, parts):
        draws = jax.random.uniform(jax.random.fold_in(jax.random.fold_in(rng, 6), axis_at), (parts,), jnp.float32, smallest / len(shards), largest / len(shards))
        return jnp.repeat(jnp.exp(draws), dims[axis_at] // parts).reshape((-1,) + (1,) * (len(dims) - axis_at - 1))

    factor_of = one(*shards[0])
    for cut in shards[1:]:
        factor_of = factor_of * one(*cut)
    return factor_of


def rank_bounds(amount, skew):
    loads = [(1 << 20) // math.isqrt(standing ** skew) + 1 for standing in range(1, amount + 1)]
    width = 1 + sum(loads) // (1 << 30)
    return np.cumsum(np.array([max(1, weight // width) for weight in loads]))


def skewed_ids(rng, extent, count, slope):
    grid = rank_bounds(count, slope)
    pick = jax.random.randint(jax.random.fold_in(rng, 1), extent, 0, int(grid[count - 1]))
    standing = jnp.searchsorted(jnp.asarray(grid, jnp.int32), pick, side="right")
    return jax.random.permutation(jax.random.fold_in(rng, 2), count)[standing].astype(jnp.int32)


def gaussian(stream_key, shape, scale, limit, shards=(), kind=jnp.bfloat16):
    values = scale * jax.random.normal(stream_key, shape, jnp.float32)
    if shards:
        values = values * shard_levels(stream_key, shape, shards, -0.22, 0.18)
    return jnp.clip(values, -limit, limit).astype(kind)


def setup_inputs(seed: int = 0) -> dict:
    streams_of = jax.random.split(jax.random.key(seed), 17)
    return {
        "token_ids": plant(skewed_ids(streams_of[0], (STEPS, SEQS), VOCAB, 2), jax.random.fold_in(streams_of[0], 3), 0, VOCAB - 1).astype(jnp.int32),
        "lengths": draw_lengths(jax.random.fold_in(streams_of[16], 71), 0),
        "embedding": gaussian(streams_of[2], (VOCAB, D), 1.0, 6.0, ((1, 4),)),
        "hyena_gain": jnp.clip(1.0 + 0.18 * jax.random.normal(streams_of[3], (D,), jnp.float32), 0.1, 1.9),
        "hyena_in": gaussian(streams_of[4], (D, 3, D), D ** -0.5, 0.0625, ((0, 4), (2, 32))),
        "fir_taps": gaussian(streams_of[5], (TAPS, 3, D), 0.5, 3.0, ((2, 32),), jnp.float32),
        "poles": jnp.clip(jnp.exp(math.log(0.995) - 1.1989602 * jax.random.uniform(streams_of[6], (STATE, D), jnp.float32) ** shard_levels(streams_of[6], (STATE, D), ((1, 32),), -0.2, 0.2)), 0.3, 0.995),
        "residues": gaussian(streams_of[7], (STATE, D), 0.3, 2.0, ((1, 32),), jnp.float32),
        "skip": jnp.clip(0.5 + 1.0 * jax.random.uniform(streams_of[8], (D,), jnp.float32) ** shard_levels(streams_of[8], (D,), ((0, 32),), -0.2, 0.2), 0.5, 1.5),
        "hyena_out": gaussian(streams_of[9], (D, D), D ** -0.5, 0.0625, ((0, 32), (1, 4))),
        "modal_state": gaussian(streams_of[10], (SEQS, STATE, D), 1.0, 6.0, ((0, 4), (2, 32)), jnp.float32),
        "fir_state": gaussian(streams_of[11], (SEQS, TAPS - 1, 3, D), 1.0, 6.0, ((0, 4), (3, 32)), jnp.float32),
        "attn_gain": jnp.clip(1.0 + 0.18 * jax.random.normal(streams_of[12], (D,), jnp.float32), 0.1, 1.9),
        "attn_in": gaussian(streams_of[13], (D, 3, D), D ** -0.5, 0.0625, ((0, 4), (2, 32))),
        "attn_out": gaussian(streams_of[14], (D, D), D ** -0.5, 0.0625, ((0, 32), (1, 4))),
        "kv_cache": draw_kv_cache(jax.random.fold_in(streams_of[16], 71), 0),
    }


EPS = 1e-06

def rms_norm(hidden, gain):
    values = hidden.astype(jnp.float32)
    total = lax.optimization_barrier(jnp.sum(values * values, axis=-1, keepdims=True))
    return (values * lax.rsqrt(total / D + EPS) * gain).astype(jnp.bfloat16)

def rotate(vectors, positions):
    half = HEAD_DIM // 2
    freqs = jnp.exp(-math.log(10000.0) * jnp.arange(half, dtype=jnp.float32) * 2.0 / HEAD_DIM)
    angles = positions.astype(jnp.float32)[:, None, None] * freqs[None, None, :]
    cosine = jnp.cos(angles)
    sine = jnp.sin(angles)
    first = vectors[..., :half]
    second = vectors[..., half:]
    return jnp.concatenate([first * cosine - second * sine, second * cosine + first * sine], axis=-1)

def attend_block(query, cache, valid_len, fresh_keys, fresh_values):
    rows, span = (cache.shape[0], cache.shape[1])
    keys = cache[:, :, 0].reshape(rows, span, HEADS, HEAD_DIM).astype(jnp.float32)
    values = cache[:, :, 1].reshape(rows, span, HEADS, HEAD_DIM).astype(jnp.float32)
    scale = 1.0 / math.sqrt(HEAD_DIM)
    scores = jnp.einsum('bhd,blhd->bhl', query.astype(jnp.float32), keys) * scale
    valid = jnp.arange(span, dtype=jnp.int32)[None, :] < valid_len[:, None]
    scores = jnp.where(valid[:, None, :], scores, -1e+30)
    fresh = jnp.einsum('bhd,bshd->bhs', query.astype(jnp.float32), fresh_keys.astype(jnp.float32)) * scale
    top = jnp.maximum(lax.optimization_barrier(jnp.max(scores, axis=2)), lax.optimization_barrier(jnp.max(fresh, axis=2)))[:, :, None]
    cache_w = jnp.exp(scores - top)
    fresh_w = jnp.exp(fresh - top)
    total = lax.optimization_barrier(jnp.sum(cache_w, axis=2, keepdims=True)) + lax.optimization_barrier(jnp.sum(fresh_w, axis=2, keepdims=True))
    cache_w = (cache_w / total).astype(jnp.bfloat16)
    fresh_w = (fresh_w / total).astype(jnp.bfloat16)
    summed = jnp.einsum('bhl,blhd->bhd', cache_w.astype(jnp.float32), values)
    summed = summed + jnp.einsum('bhs,bshd->bhd', fresh_w.astype(jnp.float32), fresh_values.astype(jnp.float32))
    return summed.reshape(rows, HEADS * HEAD_DIM).astype(jnp.bfloat16)

def attend(query, kv_cache, lengths, fresh_keys, fresh_values):
    group = 16
    count = query.shape[0] // group

    def split(array):
        return array.reshape((count, group) + array.shape[1:])

    def one_block(pieces):
        return attend_block(pieces[0], pieces[1], pieces[2], pieces[3], pieces[4])
    blocks = lax.map(one_block, (split(query), split(kv_cache), split(lengths), split(fresh_keys), split(fresh_values)))
    return blocks.reshape(query.shape[0], HEADS * HEAD_DIM)

def reference(token_ids, lengths, embedding, hyena_gain, hyena_in, fir_taps, poles, residues, skip, hyena_out, modal_state, fir_state, attn_gain, attn_in, attn_out, kv_cache):
    modal = modal_state
    fir = fir_state
    kept_keys = []
    kept_values = []
    outputs = []
    for step in range(STEPS):
        hidden0 = embedding[token_ids[step]]
        normed0 = rms_norm(hidden0, hyena_gain)
        projected = jnp.dot(normed0, hyena_in.reshape(D, 3 * D), preferred_element_type=jnp.float32).reshape(SEQS, 3, D)
        filtered = fir_taps[0] * projected + fir_taps[1] * fir[:, 0] + fir_taps[2] * fir[:, 1]
        fir = jnp.stack([projected, fir[:, 0]], axis=1)
        gated = filtered[:, 1] * filtered[:, 2]
        modal = poles * modal + gated[:, None, :]
        mixed = lax.optimization_barrier(jnp.sum(residues * modal, axis=1)) + skip * gated
        mixer = (filtered[:, 0] * mixed).astype(jnp.bfloat16)
        branch = jnp.dot(mixer, hyena_out, preferred_element_type=jnp.float32)
        hidden1 = (hidden0.astype(jnp.float32) + branch).astype(jnp.bfloat16)
        normed1 = rms_norm(hidden1, attn_gain)
        qkv = jnp.dot(normed1, attn_in.reshape(D, 3 * D), preferred_element_type=jnp.float32).astype(jnp.bfloat16)
        qkv = qkv.reshape(SEQS, 3, HEADS, HEAD_DIM)
        positions = lengths + step
        query = rotate(qkv[:, 0].astype(jnp.float32), positions).astype(jnp.bfloat16)
        key = rotate(qkv[:, 1].astype(jnp.float32), positions).astype(jnp.bfloat16)
        kept_keys.append(key)
        kept_values.append(qkv[:, 2])
        attended = attend(query, kv_cache, lengths, jnp.stack(kept_keys, axis=1), jnp.stack(kept_values, axis=1))
        branch2 = jnp.dot(attended, attn_out, preferred_element_type=jnp.float32)
        outputs.append((hidden1.astype(jnp.float32) + branch2).astype(jnp.bfloat16))
    return (jnp.stack(outputs), modal, fir)
```

```python
import math

import jax
import jax.numpy as jnp
from jax import lax
from jax.experimental import pallas as pl
from jax.experimental.pallas import tpu as pltpu
from jax.sharding import PartitionSpec as P

D = 8192
HEADS = 64
HEAD_DIM = 128
STEPS = 2
EPS = 1e-06
MESH = pl.DeviceIdType.MESH
F32 = jnp.float32
BF16 = jnp.bfloat16
HALF = 1024


def dot(a, b):
    return jnp.dot(a, b, preferred_element_type=F32)


def dot_t(a, b):
    return lax.dot_general(a, b, (((1,), (1,)), ((), ())), preferred_element_type=F32)


class Place:
    def __init__(self):
        self.w = lax.axis_index("wide")
        self.n = lax.axis_index("narrow")
        self.y = self.w // 8
        self.zl = (self.w // 4) % 2
        self.x = self.w % 4
        self.zh = self.n // 2
        self.c = self.n % 2

    def along(self, axis, step):
        y = (self.y + step) % 4 if axis == "y" else self.y
        x = (self.x + step) % 4 if axis == "x" else self.x
        zl = (self.zl + step) % 2 if axis == "zl" else self.zl
        return ((y * 2 + zl) * 4 + x, self.n)

    def narrow(self, dzh, dc):
        return (self.w, ((self.zh + dzh) % 2) * 2 + (self.c + dc) % 2)


class Sems:
    def __init__(self, send, recv):
        self.send, self.recv, self.next = send, recv, 0

    def take(self, count=1):
        first = self.next
        self.next += count
        return first

    def copy(self, src, dst, device, slot=None):
        slot = self.take() if slot is None else slot
        made = pltpu.make_async_remote_copy(
            src_ref=src,
            dst_ref=dst,
            send_sem=self.send.at[slot],
            recv_sem=self.recv.at[slot],
            device_id=device,
            device_id_type=MESH,
        )
        made.start()
        return made


def add_blocks(out, terms, blocks):
    def body(k, carry):
        total = terms[0][k].astype(F32)
        for term in terms[1:]:
            total = total + term[k].astype(F32)
        out[k] = total.astype(out.dtype)
        return carry

    lax.fori_loop(0, blocks, body, 0)


def ring_rs(place, sems, axis, me, src, recv, temp, sink, blocks):
    sent = []
    first = []
    second = []
    for s, step in enumerate((1, 3)):
        there = place.along(axis, step)
        first.append(sems.copy(src.at[(me + 2) % 4, s], recv.at[s, 0], there))
        second.append(sems.copy(src.at[(me + step) % 4, 1 - s], recv.at[s, 1], there))
    yield
    third = []
    for s, step in enumerate((1, 3)):
        there = place.along(axis, step)
        first[s].wait_recv()
        add_blocks(temp.at[s], [src.at[(me + step) % 4, s], recv.at[s, 0]], blocks)
        third.append(sems.copy(temp.at[s], recv.at[s, 2], there))
    yield
    for z in range(2):
        second[1 - z].wait_recv()
        third[z].wait_recv()
        sink(z, [src.at[me, z], recv.at[z, 2], recv.at[1 - z, 1]])
    sent = first + second + third
    yield sent


def rs_wide_part(place, sems, axes, src, bufs, out):
    recv1, temp1, mid, recv2, temp2, last, recv3 = bufs
    sent = []

    def sink1(z, terms):
        def body(q, carry):
            total = terms[0][q].astype(F32)
            for term in terms[1:]:
                total = total + term[q].astype(F32)
            mid[q, z, 0] = total.astype(BF16)
            return carry

        lax.fori_loop(0, 4, body, 0)

    def sink2(z, terms):
        total = terms[0][0].astype(F32)
        for term in terms[1:]:
            total = total + term[0].astype(F32)
        last[z] = total.astype(BF16)

    for got in ring_rs(place, sems, axes[0], getattr(place, axes[0]), src, recv1, temp1, sink1, 4):
        if got is not None:
            sent += got
        else:
            yield
    for got in ring_rs(place, sems, axes[1], getattr(place, axes[1]), mid, recv2, temp2, sink2, 1):
        if got is not None:
            sent += got
        else:
            yield
    cross = sems.copy(last.at[1 - place.zl], recv3, place.along("zl", 1))
    yield
    cross.wait_recv()
    out(last[place.zl].astype(F32) + recv3[...].astype(F32))
    for copy in sent + [cross]:
        copy.wait_send()


def ag_wide_part(place, sems, axes, held):
    first, second = axes
    f, s, zl = getattr(place, first), getattr(place, second), place.zl
    sent = []
    own = held.at[f, zl, s]
    base = sems.take(4)
    near = []
    cross = sems.copy(own, own, place.along("zl", 1))
    for d, step in enumerate((1, 3)):
        sems.copy(own, own, place.along(second, step), base + d * 2 + zl)
    yield
    cross.wait_recv()
    other = held.at[f, 1 - zl, s]
    for d, step in enumerate((1, 3)):
        sems.copy(other, other, place.along(second, step), base + d * 2 + 1 - zl)
    for d, step in enumerate((1, 3)):
        for z in range(2):
            block = held.at[f, z, s]
            near.append(
                pltpu.make_async_remote_copy(
                    src_ref=block,
                    dst_ref=block,
                    send_sem=sems.send.at[base + d * 2 + z],
                    recv_sem=sems.recv.at[base + d * 2 + z],
                    device_id=place.along(second, step),
                    device_id_type=MESH,
                )
            )
    yield
    far = []
    for d, step in enumerate((1, 3)):
        near[d * 2 + d].wait_recv()
        block = held.at[f, d, (s - step) % 4]
        far.append(sems.copy(block, block, place.along(second, step)))
    yield
    near[1].wait_recv()
    near[2].wait_recv()
    far[0].wait_recv()
    far[1].wait_recv()
    near2 = []
    for z in range(2):
        for d, step in enumerate((1, 3)):
            block = held.at[f, z]
            near2.append(sems.copy(block, block, place.along(first, step)))
    yield
    far2 = []
    for d, step in enumerate((1, 3)):
        near2[d * 2 + d].wait_recv()
        block = held.at[(f - step) % 4, d]
        far2.append(sems.copy(block, block, place.along(first, step)))
    yield
    near2[1].wait_recv()
    near2[2].wait_recv()
    far2[0].wait_recv()
    far2[1].wait_recv()
    for copy in [cross] + near + far + near2 + far2:
        copy.wait_send()


def interleave(*parts):
    parts = list(parts)
    while parts:
        left = []
        for part in parts:
            try:
                next(part)
                left.append(part)
            except StopIteration:
                pass
        parts = left


def rs_narrow(place, sems, src, core_recv, temp, z_recv):
    zh, c = place.zh, place.c
    mate = place.narrow(0, 1)
    far = sems.copy(src.at[(1 - zh) * 2 + 1 - c], core_recv.at[0], mate)
    near = sems.copy(src.at[zh * 2 + 1 - c], core_recv.at[1], mate)
    far.wait_recv()
    add_blocks(temp, [src.at[(1 - zh) * 2 + c], core_recv.at[0]], temp.shape[0])
    cross = sems.copy(temp, z_recv, place.narrow(1, 0))
    near.wait_recv()
    cross.wait_recv()
    for copy in (far, near, cross):
        copy.wait_send()
    return [src.at[zh * 2 + c], core_recv.at[1], z_recv]


def ag_narrow(place, sems, held):
    zh, c = place.zh, place.c
    own = held.at[place.n]
    cross = sems.copy(own, own, place.narrow(1, 0))
    near = sems.copy(own, own, place.narrow(0, 1))
    cross.wait_recv()
    got = held.at[(1 - zh) * 2 + c]
    handed = sems.copy(got, got, place.narrow(0, 1))
    near.wait_recv()
    handed.wait_recv()
    for copy in (cross, near, handed):
        copy.wait_send()


def all_to_all(place, sems, src, dst):
    base = sems.take(32)

    def copy_of(d):
        peer = (place.w + d) % 32
        return pltpu.make_async_remote_copy(
            src_ref=src.at[peer],
            dst_ref=dst.at[place.w],
            send_sem=sems.send.at[base + d],
            recv_sem=sems.recv.at[base + d],
            device_id=(peer, place.n),
            device_id_type=MESH,
        )

    def begin(d, carry):
        copy_of(d).start()
        return carry

    def end(d, carry):
        copy_of(d).wait()
        return carry

    lax.fori_loop(1, 32, begin, 0)
    dst[place.w] = src[place.w]
    return lambda: lax.fori_loop(1, 32, end, 0)


def share_scales(place, sems, sums, got, scales):
    copies = []
    for k, (dzh, dc) in enumerate(((0, 1), (1, 0), (1, 1))):
        copies.append(sems.copy(sums, got.at[k], place.narrow(dzh, dc)))

    def finish():
        for copy in copies:
            copy.wait()
        total = sums[...] + got[0] + got[1] + got[2]
        scales[...] = lax.rsqrt(total / D + EPS)

    return finish


def project_out(rows, weights, parts):
    def body(y, carry):
        block = rows[pl.ds(pl.multiple_of(y * 128, 128), 128), :]
        a = dot(block, weights[:, :HALF]).astype(BF16).reshape(2, 4, 16, HALF)
        parts[0][y] = a
        b = dot(block, weights[:, HALF:]).astype(BF16).reshape(2, 4, 16, HALF)
        for x in range(4):
            parts[1][x, :, y] = b[:, x]
        return carry

    lax.fori_loop(0, 4, body, 0)


def kernel(
    tok_ref,
    hyena_gain_ref,
    attn_gain_ref,
    taps_ref,
    poles_ref,
    residues_ref,
    skip_ref,
    fir_ref,
    cos_ref,
    sin_ref,
    len_ref,
    emb_hbm,
    hyena_in_hbm,
    modal_hbm,
    hyena_out_hbm,
    attn_in_hbm,
    attn_out_hbm,
    kv_hbm,
    out_ref,
    modal_out_hbm,
    fir_out_ref,
    emb,
    hyena_in,
    modal,
    hyena_out,
    attn_in,
    attn_out,
    kv_raw,
    load_sem,
    send_sem,
    recv_sem,
    tokens,
    xg,
    table,
    zsend,
    zcore,
    ztemp,
    zrecv,
    sums,
    sums_got,
    scales,
    mixers,
    psend,
    r1,
    t1,
    m1,
    r2,
    t2,
    l2,
    r3,
    hidden0,
    hidden1,
    held,
    qkv,
    spread,
    spread16,
    routed,
    att_send,
    att_recv,
    att_rows,
    att_full,
):
    place = Place()
    sems = Sems(send_sem, recv_sem)
    w, n = place.w, place.n

    barrier = pltpu.get_barrier_semaphore()

    def greet(d, carry):
        pl.semaphore_signal(
            barrier, inc=1, device_id=((w + d) % 32, n), device_id_type=MESH
        )
        return carry

    lax.fori_loop(1, 32, greet, 0)
    for dzh, dc in ((0, 1), (1, 0), (1, 1)):
        pl.semaphore_signal(barrier, inc=1, device_id=place.narrow(dzh, dc), device_id_type=MESH)

    loads = []
    for k, (src, dst) in enumerate(
        (
            (emb_hbm, emb),
            (hyena_in_hbm, hyena_in),
            (modal_hbm, modal),
            (hyena_out_hbm, hyena_out),
            (attn_in_hbm, attn_in),
            (attn_out_hbm, attn_out),
        )
    ):
        copy = pltpu.make_async_copy(src, dst, load_sem.at[k])
        copy.start()
        loads.append(copy)

    loads[0].wait()

    def gain_rows(k, carry):
        rows = pl.ds(pl.multiple_of(k * 64, 64), 64)
        xg[rows, :] = (emb[rows, :].astype(F32) * hyena_gain_ref[...]).astype(BF16)
        return carry

    lax.fori_loop(0, 8, gain_rows, 0)
    sums[0] = dot_t(jnp.ones((8, 2048), BF16), emb[...] * emb[...])

    pl.semaphore_wait(barrier, 34)

    tokens[w] = tok_ref[...]
    base = sems.take(32)

    def token_copy(d):
        return pltpu.make_async_remote_copy(
            src_ref=tok_ref,
            dst_ref=tokens.at[w],
            send_sem=send_sem.at[base + d],
            recv_sem=recv_sem.at[base + d],
            device_id=((w + d) % 32, n),
            device_id_type=MESH,
        )

    def token_start(d, carry):
        token_copy(d).start()
        return carry

    def token_wait(d, carry):
        token_copy(d).wait()
        return carry

    lax.fori_loop(1, 32, token_start, 0)
    scales_ready = share_scales(place, sems, sums.at[0], sums_got.at[0], scales.at[0])

    def load_kv(h, carry):
        for j in range(2):
            lanes = pl.ds(pl.multiple_of(h * 128, 128), 128)
            pltpu.make_async_copy(kv_hbm.at[j, :, :, lanes], kv_raw.at[j, h], load_sem.at[6]).start()
        return carry

    loads[1].wait()
    lax.fori_loop(0, 64, load_kv, 0)

    def project(k, carry):
        c, m = k // 2, k % 2
        rows = pl.ds(pl.multiple_of(m * 256, 256), 256)
        table[c, rows, :] = dot(xg[rows, :], hyena_in[c]).astype(BF16)
        return carry

    lax.fori_loop(0, 6, project, 0)

    lax.fori_loop(1, 32, token_wait, 0)
    token_rows = tokens[...].reshape(256, 128)
    vocab = lax.broadcasted_iota(jnp.int32, (64, 512), 1)
    for t in range(STEPS):
        for m in range(4):
            hot = (token_rows[m * 64 : (m + 1) * 64, t * 64 : t * 64 + 1] == vocab).astype(F32).astype(BF16)
            for c in range(3):
                picked = dot(hot, table[c])
                zsend[m, t * 4 : t * 4 + 4, :, c * 256 : (c + 1) * 256] = picked.astype(BF16).reshape(
                    4, 16, 256
                )

    terms = rs_narrow(place, sems, zsend, zcore.at[0], ztemp.at[0], zrecv.at[0])
    scales_ready()

    mine = jnp.concatenate([tok_ref[:, 0:1], tok_ref[:, 64:65]], axis=0)
    hot16 = (mine == lax.broadcasted_iota(jnp.int32, (16, 512), 1)).astype(F32).astype(BF16)
    hidden0[...] = dot(hot16, emb[...])

    loads[2].wait()
    poles = poles_ref[...][None]
    residues = residues_ref[...][None]
    vocab8 = lax.broadcasted_iota(jnp.int32, (8, 512), 1)

    def filters(g, carry):
        rows = pl.ds(pl.multiple_of(g * 8, 8), 8)
        own_tokens = tokens[n * 8 + g]
        projected = []
        for t in range(STEPS):
            picked = jnp.where(own_tokens[:, t * 64 : t * 64 + 1] == vocab8, scales[0], 0.0)
            scale = jnp.sum(picked, axis=1, keepdims=True)
            projected.append(qkv[pl.ds(pl.multiple_of(t * 64 + g * 8, 8), 8), :] * scale)
        fir0 = [fir_ref[0, c, rows, :] for c in range(3)]
        fir1 = [fir_ref[1, c, rows, :] for c in range(3)]
        proj = [[projected[t][:, c * 256 : (c + 1) * 256] for c in range(3)] for t in range(2)]
        step0 = [
            taps_ref[c : c + 1, :] * proj[0][c]
            + taps_ref[3 + c : 4 + c, :] * fir0[c]
            + taps_ref[6 + c : 7 + c, :] * fir1[c]
            for c in range(3)
        ]
        step1 = [
            taps_ref[c : c + 1, :] * proj[1][c]
            + taps_ref[3 + c : 4 + c, :] * proj[0][c]
            + taps_ref[6 + c : 7 + c, :] * fir0[c]
            for c in range(3)
        ]
        for c in range(3):
            fir_out_ref[0, c, rows, :] = proj[1][c]
            fir_out_ref[1, c, rows, :] = proj[0][c]
        state = modal[rows]
        mixer = []
        for step in (step0, step1):
            gated = step[1] * step[2]
            state = poles * state + gated[:, None, :]
            mixed = jnp.sum(residues * state, axis=1) + skip_ref[...] * gated
            mixer.append(step[0] * mixed)
        modal[rows] = state
        mixers[n, g] = jnp.concatenate(mixer, axis=0).astype(BF16)
        return carry

    def sum_terms(k, carry):
        total = terms[0][k].astype(F32) + terms[1][k].astype(F32) + terms[2][k].astype(F32)
        qkv[pl.ds(pl.multiple_of(k * 16, 16), 16), :] = total
        return carry

    lax.fori_loop(0, 8, sum_terms, 0)
    lax.fori_loop(0, 8, filters, 0)
    modal_store = pltpu.make_async_copy(modal, modal_out_hbm, load_sem.at[7])
    modal_store.start()
    ag_narrow(place, sems, mixers)

    def out_projection(k, rows, weights, sink):
        project_out(rows, weights, [psend.at[k, 0], psend.at[k, 1]])
        gens = []
        for p, axes in enumerate((("y", "x"), ("x", "y"))):
            bufs = (
                r1.at[k, p], t1.at[k, p], m1.at[k, p], r2.at[k, p], t2.at[k, p], l2.at[k, p], r3.at[k, p],
            )
            gens.append(rs_wide_part(place, sems, axes, psend.at[k, p], bufs, sink(p)))
        interleave(*gens)

    loads[3].wait()
    zl, x, y = place.zl, place.x, place.y

    def sink_hidden(p):
        def sink(total):
            cols = pl.ds(p * HALF, HALF)
            hidden1[p] = (hidden0[:, cols] + total).astype(BF16)

        return sink

    out_projection(0, mixers.reshape(512, 256), hyena_out, sink_hidden)
    held[0, y, zl, x] = hidden1[0]
    held[1, x, zl, y] = hidden1[1]
    interleave(
        ag_wide_part(place, sems, ("y", "x"), held.at[0]),
        ag_wide_part(place, sems, ("x", "y"), held.at[1]),
    )

    loads[4].wait()

    def gather_rows(k, carry):
        a = held[0, k // 8, (k // 4) % 2, k % 4]
        b = held[1, k % 4, (k // 4) % 2, k // 8]
        both = jnp.concatenate([a, b], axis=1).astype(F32)
        rows = pl.ds(pl.multiple_of(k * 16, 16), 16)
        emb[rows, :] = (both * both).astype(BF16)
        xg[rows, :] = (both * attn_gain_ref[...]).astype(BF16)
        return carry

    lax.fori_loop(0, 32, gather_rows, 0)
    sums[1] = dot_t(jnp.ones((8, 2048), BF16), emb[...])
    scales_ready = share_scales(place, sems, sums.at[1], sums_got.at[1], scales.at[1])

    for c in range(3):

        def project_qkv(m, carry):
            rows = pl.ds(pl.multiple_of(m * 256, 256), 256)
            got = dot(xg[rows, :], attn_in[c])
            spread[2 * c, rows, :] = got[:, :128]
            spread[2 * c + 1, rows, :] = got[:, 128:]
            return carry

        lax.fori_loop(0, 2, project_qkv, 0)
    for m in range(4):
        for t in range(2):
            for j in range(2):
                for c in range(3):
                    for half in range(2):
                        piece = spread[2 * c + half, pl.ds(t * 8 + m * 2 + j, 32, stride=16), :]
                        first = (t * 2 + j) * 2
                        zsend2 = piece.astype(BF16).reshape(2, 16, 128)
                        att_lanes = slice(c * 256 + half * 128, c * 256 + half * 128 + 128)
                        zsend_b = zsend.at[4 + m]
                        zsend_b[first : first + 2, :, att_lanes] = zsend2
    terms = rs_narrow(place, sems, zsend.at[pl.ds(4, 4)], zcore.at[1], ztemp.at[1], zrecv.at[1])
    scales_ready()

    spread[0:2] = jnp.zeros((2, 512, 128), F32)
    for tj in range(4):
        t, j = tj // 2, tj % 2
        lane = lax.broadcasted_iota(jnp.int32, (32, 512), 1)
        row = lax.broadcasted_iota(jnp.int32, (32, 512), 0)
        wanted = row * 16 + t * 8 + n * 2 + j
        scale = jnp.sum(jnp.where(lane == wanted, scales[1][0:1, :], 0.0), axis=1, keepdims=True)
        rows = slice(tj * 2, tj * 2 + 2)
        total = (
            terms[0][rows].astype(F32) + terms[1][rows].astype(F32) + terms[2][rows].astype(F32)
        ).reshape(32, 768) * scale
        for c in range(3):
            at = j * 8 + (t if c == 0 else 4 + 2 * t + (c - 1))
            for half in range(2):
                lo = c * 256 + half * 128
                spread[half, pl.ds(at, 32, stride=16), :] = total[:, lo : lo + 128]

    def pack(k, carry):
        rows = pl.ds(pl.multiple_of(k * 16, 16), 16)
        both = jnp.concatenate([spread[0, rows, :], spread[1, rows, :]], axis=1)
        spread16[k] = both.astype(BF16)
        return carry

    lax.fori_loop(0, 32, pack, 0)
    routed_ready = all_to_all(place, sems, spread16, routed)
    pltpu.make_async_copy(kv_raw, kv_raw, load_sem.at[6]).wait()
    kv = kv_raw.reshape(2, 64, 128, 128)
    routed_ready()

    cos, sin = cos_ref[...], sin_ref[...]
    lane = lax.broadcasted_iota(jnp.int32, (16, 128), 1)
    row = lax.broadcasted_iota(jnp.int32, (16, 128), 0)
    position = lane // 2
    valid = (lane % 2 == 0) & (
        (position < len_ref[...])
        | (position == 62)
        | ((position == 63) & (row % 8 == 1))
    )
    top_rows = lax.broadcasted_iota(jnp.int32, (8, 128), 0)
    inv = 1.0 / math.sqrt(HEAD_DIM)

    def attend(k, carry):
        message = jnp.zeros((8, 128), F32)
        for hh in range(2):
            h = k * 2 + hh
            vectors = routed[k, :, hh * 128 : hh * 128 + 128].astype(F32)
            turned = vectors * cos + pltpu.roll(vectors, 64, axis=1) * sin
            turned16 = turned.astype(BF16)
            scores = []
            for j in range(2):
                old = kv[j, h, 112:128, :].astype(F32)
                fresh = jnp.where(top_rows >= 4, turned[j * 8 : j * 8 + 8], old[8:16])
                kv[j, h, 112:128, :] = jnp.concatenate([old[0:8], fresh], axis=0).astype(BF16)
                scores.append(dot_t(turned16, kv[j, h])[j * 8 : j * 8 + 8])
            score = jnp.where(valid, jnp.concatenate(scores, axis=0) * inv, -1e30)
            grown = jnp.exp(score - jnp.max(score, axis=1, keepdims=True))
            weight = grown / jnp.sum(grown, axis=1, keepdims=True)
            weight16 = pltpu.roll(weight, 1, axis=1).astype(BF16)
            for j in range(2):
                got = dot(weight16, kv[j, h])[j * 8 : j * 8 + 8]
                at = hh * 4 + j * 2
                moved = pltpu.roll(got, at, axis=0) if at else got
                message = jnp.where((top_rows >= at) & (top_rows < at + 2), moved, message)
        att_send[k] = message.astype(BF16).astype(F32)
        return carry

    lax.fori_loop(0, 32, attend, 0)
    all_to_all(place, sems, att_send, att_recv)()
    flat = att_recv.reshape(256, 128)
    for jt in range(4):
        for hh in range(2):
            piece = flat[pl.ds(hh * 4 + jt, 32, stride=8), :]
            att_rows[n, jt * 2 : jt * 2 + 2, :, hh * 128 : hh * 128 + 128] = piece.astype(BF16).reshape(
                2, 16, 128
            )
    ag_narrow(place, sems, att_rows)
    for m in range(4):
        for jt in range(4):
            j, t = jt // 2, jt % 2
            for hh in range(2):
                piece = att_rows[m, jt * 2 : jt * 2 + 2, :, hh * 128 : hh * 128 + 128].astype(F32)
                spread[hh, pl.ds(t * 8 + m * 2 + j, 32, stride=16), :] = piece.reshape(32, 128)

    def pack_rows(k, carry):
        rows = pl.ds(pl.multiple_of(k * 64, 64), 64)
        both = jnp.concatenate([spread[0, rows, :], spread[1, rows, :]], axis=1)
        att_full[rows, :] = both.astype(BF16)
        return carry

    lax.fori_loop(0, 8, pack_rows, 0)
    loads[5].wait()

    def sink_out(p):
        def sink(total):
            cols = pl.ds(p * HALF, HALF)
            out_ref[:, cols] = (hidden1[p].astype(F32) + total).astype(BF16)

        return sink

    out_projection(1, att_full, attn_out, sink_out)
    modal_store.wait()


def local(
    token_ids,
    lengths,
    embedding,
    hyena_gain,
    hyena_in,
    fir_taps,
    poles,
    residues,
    skip,
    hyena_out,
    modal_state,
    fir_state,
    attn_gain,
    attn_in,
    attn_out,
    kv_cache,
):
    tok = jnp.repeat(token_ids.T, 64, axis=1)
    half = HEAD_DIM // 2
    freqs = jnp.exp(-math.log(10000.0) * jnp.arange(half, dtype=F32) * 2.0 / HEAD_DIM)
    step = jnp.array([0, 1, 0, 0, 0, 0, 1, 0], jnp.int32)
    turns = jnp.array([1, 1, 0, 0, 1, 0, 1, 0], F32)
    angles = ((lengths[:, None] + step[None, :]).astype(F32) * turns[None, :])[..., None] * freqs
    cosine = jnp.cos(angles).reshape(16, half)
    sine = jnp.sin(angles).reshape(16, half)
    cos = jnp.concatenate([cosine, cosine], axis=1)
    sin = jnp.concatenate([-sine, sine], axis=1)
    lens = jnp.broadcast_to(lengths[:, None, None], (2, 8, 128)).reshape(16, 128)
    vmem = pl.BlockSpec(memory_space=pltpu.VMEM)
    anywhere = pl.BlockSpec(memory_space=pl.ANY)

    out, modal_out, fir_out = pl.pallas_call(
        kernel,
        out_shape=(
            jax.ShapeDtypeStruct((16, 2048), BF16),
            jax.ShapeDtypeStruct((64, 16, 256), F32),
            jax.ShapeDtypeStruct((2, 3, 64, 256), F32),
        ),
        in_specs=[vmem] * 11 + [anywhere] * 7,
        out_specs=(vmem, anywhere, vmem),
        scratch_shapes=[
            pltpu.VMEM((512, 2048), BF16),
            pltpu.VMEM((3, 2048, 256), BF16),
            pltpu.VMEM((64, 16, 256), F32),
            pltpu.VMEM((256, 2048), BF16),
            pltpu.VMEM((3, 2048, 256), BF16),
            pltpu.VMEM((256, 2048), BF16),
            pltpu.VMEM((2, 64, 64, 2, 128), BF16),
            pltpu.SemaphoreType.DMA((8,)),
            pltpu.SemaphoreType.DMA((256,)),
            pltpu.SemaphoreType.DMA((256,)),
            pltpu.VMEM((32, 8, 128), jnp.int32),
            pltpu.VMEM((512, 2048), BF16),
            pltpu.VMEM((3, 512, 256), BF16),
            pltpu.VMEM((8, 8, 16, 768), BF16),
            pltpu.VMEM((2, 2, 8, 16, 768), BF16),
            pltpu.VMEM((2, 8, 16, 768), BF16),
            pltpu.VMEM((2, 8, 16, 768), BF16),
            pltpu.VMEM((2, 8, 512), F32),
            pltpu.VMEM((2, 3, 8, 512), F32),
            pltpu.VMEM((2, 8, 512), F32),
            pltpu.VMEM((4, 8, 16, 256), BF16),
            pltpu.VMEM((2, 2, 4, 2, 4, 16, HALF), BF16),
            pltpu.VMEM((2, 2, 2, 3, 4, 16, HALF), BF16),
            pltpu.VMEM((2, 2, 2, 4, 16, HALF), BF16),
            pltpu.VMEM((2, 2, 4, 2, 1, 16, HALF), BF16),
            pltpu.VMEM((2, 2, 2, 3, 1, 16, HALF), BF16),
            pltpu.VMEM((2, 2, 2, 1, 16, HALF), BF16),
            pltpu.VMEM((2, 2, 2, 16, HALF), BF16),
            pltpu.VMEM((2, 2, 16, HALF), BF16),
            pltpu.VMEM((16, 2048), F32),
            pltpu.VMEM((2, 16, HALF), BF16),
            pltpu.VMEM((2, 4, 2, 4, 16, HALF), BF16),
            pltpu.VMEM((128, 768), F32),
            pltpu.VMEM((6, 512, 128), F32),
            pltpu.VMEM((32, 16, 256), BF16),
            pltpu.VMEM((32, 16, 256), BF16),
            pltpu.VMEM((32, 8, 128), F32),
            pltpu.VMEM((32, 8, 128), F32),
            pltpu.VMEM((4, 8, 16, 256), BF16),
            pltpu.VMEM((512, 256), BF16),
        ],
        compiler_params=pltpu.CompilerParams(
            collective_id=0, has_side_effects=True, vmem_limit_bytes=56 * 1024 * 1024
        ),
        name="decode",
    )(
        tok,
        hyena_gain[None, :],
        attn_gain[None, :],
        fir_taps.reshape(9, 256),
        poles,
        residues,
        skip[None, :],
        fir_state.transpose(1, 2, 0, 3),
        cos,
        sin,
        lens,
        embedding,
        hyena_in.transpose(1, 0, 2),
        modal_state,
        hyena_out,
        attn_in.transpose(1, 0, 2),
        attn_out,
        kv_cache,
    )
    return out.reshape(2, 8, 2048), modal_out, fir_out.transpose(2, 0, 1, 3)


def solution(mesh):
    placed = (
        P(None, "wide"),
        P(("wide", "narrow")),
        P(None, "narrow"),
        P("narrow"),
        P("narrow", None, "wide"),
        P(None, None, "wide"),
        P(None, "wide"),
        P(None, "wide"),
        P("wide"),
        P("wide", "narrow"),
        P("narrow", None, "wide"),
        P("narrow", None, None, "wide"),
        P("narrow"),
        P("narrow", None, "wide"),
        P("wide", "narrow"),
        P(("wide", "narrow"), None, None, None),
    )
    return jax.shard_map(
        local,
        mesh=mesh,
        in_specs=placed,
        out_specs=(
            P(None, "wide", "narrow"),
            P("narrow", None, "wide"),
            P("narrow", None, None, "wide"),
        ),
        check_vma=False,
    )
```

```python
import math

import jax
import jax.numpy as jnp
from jax import lax
from jax.experimental import pallas as pl
from jax.experimental.pallas import tpu as pltpu
from jax.sharding import PartitionSpec as P

D = 8192
HEADS = 64
HEAD_DIM = 128
STEPS = 2
EPS = 1e-06
MESH = pl.DeviceIdType.MESH
F32 = jnp.float32
BF16 = jnp.bfloat16
HALF = 1024


def dot(a, b):
    return jnp.dot(a, b, preferred_element_type=F32)


def dot_t(a, b):
    return lax.dot_general(a, b, (((1,), (1,)), ((), ())), preferred_element_type=F32)


class Place:
    def __init__(self):
        self.w = lax.axis_index("wide")
        self.n = lax.axis_index("narrow")
        self.y = self.w // 8
        self.zl = (self.w // 4) % 2
        self.x = self.w % 4
        self.zh = self.n // 2
        self.c = self.n % 2

    def along(self, axis, step):
        y = (self.y + step) % 4 if axis == "y" else self.y
        x = (self.x + step) % 4 if axis == "x" else self.x
        zl = (self.zl + step) % 2 if axis == "zl" else self.zl
        return ((y * 2 + zl) * 4 + x, self.n)

    def shifted(self, axis, step, dzl):
        y = (self.y + step) % 4 if axis == "y" else self.y
        x = (self.x + step) % 4 if axis == "x" else self.x
        return ((y * 2 + (self.zl + dzl) % 2) * 4 + x, self.n)

    def narrow(self, dzh, dc):
        return (self.w, ((self.zh + dzh) % 2) * 2 + (self.c + dc) % 2)


class Sems:
    def __init__(self, send, recv):
        self.send, self.recv, self.sends, self.recvs = send, recv, 0, 0

    def sender(self):
        self.sends += 1
        return self.send.at[self.sends - 1]

    def receiver(self):
        self.recvs += 1
        return self.recv.at[self.recvs - 1]


def push(src, dst, send_sem, recv_sem, device):
    pltpu.make_async_remote_copy(
        src_ref=src,
        dst_ref=dst,
        send_sem=send_sem,
        recv_sem=recv_sem,
        device_id=device,
        device_id_type=MESH,
    ).start()


def drain(sem, like):
    pltpu.make_async_copy(like, like, sem).wait()


def total_of(*terms):
    total = terms[0].astype(F32)
    for term in terms[1:]:
        total = total + term.astype(F32)
    return total


def rs_wide_part(place, sems, axes, src, bufs, fill, out):
    far, close, temp, mid, inbox = bufs
    send_sem, far_sem, close_sem, in_sem = sems
    first, second = axes
    f, s = getattr(place, first), getattr(place, second)
    zs = (place.zl, 1 - place.zl)
    steps = (1, 3)

    def block(step, h, o):
        return ((f + step) % 4) * 8 + zs[h] * 4 + (s + o) % 4

    def hand_on(o):
        drain(far_sem.at[o], far.at[o])
        for h in (1, 0):
            temp[o, h] = total_of(src[block(steps[h], h, o)], far[o, h]).astype(BF16)
            push(temp.at[o, h], close.at[o, h], send_sem, close_sem.at[o], place.along(first, steps[h]))

    def send_close(o):
        for h in (1, 0):
            step = steps[1 - h]
            push(src.at[block(step, h, o)], close.at[o, 2 + h], send_sem, close_sem.at[o], place.along(first, step))

    def finish(o):
        drain(close_sem.at[o], close.at[o])
        for h in (1, 0):
            total = total_of(src[block(0, h, o)], close[o, h], close[o, 2 + h])
            if h or o:
                mid[h * 4 + o] = total.astype(BF16)
                there = place.shifted(second, o, h)
                push(mid.at[h * 4 + o], inbox.at[h * 4 + o], send_sem, in_sem, there)
        return total

    fill((f + 2) % 4)
    for o in (2, 1, 3, 0):
        for h in (1, 0):
            push(src.at[block(2, h, o)], far.at[o, h], send_sem, far_sem.at[o], place.along(first, steps[h]))
    yield
    fill((f + 1) % 4)
    fill((f + 3) % 4)
    send_close(2)
    yield
    hand_on(2)
    send_close(1)
    send_close(3)
    yield
    fill(f)
    hand_on(1)
    hand_on(3)
    send_close(0)
    yield
    hand_on(0)
    yield
    finish(2)
    yield
    finish(1)
    finish(3)
    yield
    total = finish(0)
    yield
    drain(in_sem, inbox.at[pl.ds(1, 7)])
    for k in range(1, 8):
        total = total + inbox[k].astype(F32)
    out(total)
    drain(send_sem, src.at[pl.ds(0, 31)])


def ag_wide_part(place, sems, axes, held):
    first, second = axes
    f, s = getattr(place, first), getattr(place, second)
    zs = (place.zl, 1 - place.zl)
    steps = (1, 3)
    send_sem, in_sem, pass_sem, end_sem = sems

    def block(step, h, o):
        return held.at[((f + step) % 4) * 8 + zs[h] * 4 + (s + o) % 4]

    def ring(h, o):
        for d, step in enumerate(steps):
            sem = pass_sem.at[h * 4 + o] if d == h else end_sem
            push(block(0, h, o), block(0, h, o), send_sem, sem, place.along(first, step))

    def arrive(h, o):
        drain(in_sem.at[h * 4 + o], block(0, h, o))
        ring(h, o)

    def pass_on(h, o):
        drain(pass_sem.at[h * 4 + o], block(0, h, o))
        got = block(4 - steps[h], h, o)
        push(got, got, send_sem, end_sem, place.along(first, steps[h]))

    own = block(0, 0, 0)
    order = ((1, 0), (0, 1), (0, 3), (1, 1), (1, 3), (0, 2), (1, 2))
    for h, o in order:
        push(own, own, send_sem, in_sem.at[h * 4 + (4 - o) % 4], place.shifted(second, o, h))
        if (h, o) == (0, 3):
            ring(0, 0)
    yield
    arrive(1, 0)
    yield
    arrive(0, 1)
    arrive(0, 3)
    yield
    pass_on(0, 0)
    yield
    arrive(1, 1)
    arrive(1, 3)
    yield
    pass_on(1, 0)
    yield
    arrive(0, 2)
    arrive(1, 2)
    yield
    for h, o in ((0, 1), (0, 3), (1, 1), (1, 3)):
        pass_on(h, o)
    yield
    for h, o in ((0, 2), (1, 2)):
        pass_on(h, o)
    yield
    drain(end_sem, held.at[pl.ds(0, 16)])
    drain(send_sem, held.at[pl.ds(0, 31)])


def interleave(*parts):
    parts = list(parts)
    while parts:
        left = []
        for part in parts:
            try:
                next(part)
                left.append(part)
            except StopIteration:
                pass
        parts = left


def rs_narrow(place, sems, src, fill, core_recv, temp, z_recv):
    zh, c = place.zh, place.c
    mate, across = place.narrow(0, 1), place.narrow(1, 0)
    parts = [pl.ds(p * 4, 4) for p in range(2)]
    send_sem, near_sem = sems.sender(), sems.receiver()
    far_sems = [sems.receiver() for p in parts]
    cross_sems = [sems.receiver() for p in parts]
    over = (1 - zh) * 2 + 1 - c
    fill(over)
    for p, far_sem in zip(parts, far_sems):
        push(src.at[over, p], core_recv.at[0, p], send_sem, far_sem, mate)
    over = (1 - zh) * 2 + c
    fill(over)
    for p, far_sem, cross_sem in zip(parts, far_sems, cross_sems):
        drain(far_sem, temp.at[p])
        temp[p] = total_of(src[over, p], core_recv[0, p]).astype(BF16)
        push(temp.at[p], z_recv.at[p], send_sem, cross_sem, across)
    fill(zh * 2 + 1 - c)
    push(src.at[zh * 2 + 1 - c], core_recv.at[1], send_sem, near_sem, mate)
    fill(zh * 2 + c)
    drain(near_sem, z_recv)
    for p, cross_sem in zip(parts, cross_sems):
        drain(cross_sem, z_recv.at[p])
    drain(send_sem, src.at[pl.ds(0, 3)])
    return [src.at[zh * 2 + c], core_recv.at[1], z_recv]


def ag_narrow(place, sems, held):
    zh, c = place.zh, place.c
    own = held.at[place.n]
    send_sem, cross_sem, core_sem = sems.sender(), sems.receiver(), sems.receiver()
    push(own, own, send_sem, cross_sem, place.narrow(1, 0))
    push(own, own, send_sem, core_sem, place.narrow(0, 1))
    drain(cross_sem, own)
    got = held.at[(1 - zh) * 2 + c]
    push(got, got, send_sem, core_sem, place.narrow(0, 1))
    drain(core_sem, held.at[pl.ds(0, 2)])
    drain(send_sem, held.at[pl.ds(0, 3)])


def share_scales(place, sems, sums, got, scales):
    send_sem, recv_sem = sems.sender(), sems.receiver()
    for k, (dzh, dc) in enumerate(((0, 1), (1, 0), (1, 1))):
        push(sums, got.at[k], send_sem, recv_sem, place.narrow(dzh, dc))

    def finish():
        drain(recv_sem, got)
        drain(send_sem, got)
        total = sums[...] + got[0] + got[1] + got[2]
        scales[...] = lax.rsqrt(total / D + EPS)

    return finish


def kernel(
    tok_ref,
    len_ref,
    hyena_gain_ref,
    attn_gain_ref,
    taps_ref,
    poles_ref,
    residues_ref,
    skip_ref,
    fir_hbm,
    emb_hbm,
    hyena_in_hbm,
    modal_hbm,
    hyena_out_hbm,
    attn_in_hbm,
    attn_out_hbm,
    kv_hbm,
    out_ref,
    modal_out_hbm,
    fir_out_hbm,
    emb,
    hyena_in,
    modal,
    hyena_out,
    attn_in,
    attn_out,
    kv_raw,
    fir_raw,
    load_sem,
    send_sem,
    recv_sem,
    rs_sem,
    ag_sem,
    tokens,
    xg,
    table,
    zsend,
    zcore,
    ztemp,
    zrecv,
    sums,
    sums_got,
    scales,
    mixers,
    psend,
    far,
    close,
    temp,
    mid,
    inbox,
    hidden0,
    hidden1,
    held,
    qkv,
    wide_qkv,
    spread,
    spread16,
    routed,
    turned16,
    scored,
    weights16,
    att_send,
    att_recv,
    att_rows,
    att_full,
):
    place = Place()
    sems = Sems(send_sem, recv_sem)
    w, n = place.w, place.n

    barrier = pltpu.get_barrier_semaphore()

    def peer(d):
        return ((w + d) % 32, ((place.zh + d // 32) % 2) * 2 + place.c)

    def greet(d, carry):
        pl.semaphore_signal(barrier, inc=1, device_id=peer(d), device_id_type=MESH)
        return carry

    lax.fori_loop(1, 64, greet, 0)
    for dzh in range(2):
        pl.semaphore_signal(barrier, inc=1, device_id=place.narrow(dzh, 1), device_id_type=MESH)

    loads = []
    for k, (src, dst) in enumerate(
        (
            (emb_hbm, emb),
            (hyena_in_hbm, hyena_in),
            (modal_hbm, modal),
            (hyena_out_hbm, hyena_out),
            (attn_in_hbm, attn_in),
            (attn_out_hbm, attn_out),
        )
    ):
        copy = pltpu.make_async_copy(src, dst, load_sem.at[k])
        loads.append(copy)
    loads[0].start()
    loads[1].start()
    loads[2].start()
    fir = fir_raw.reshape(6, 128, 128)
    for c in range(3):
        for half in range(2):
            pltpu.make_async_copy(
                fir_hbm.at[:, c, :, pl.ds(half * 128, 128)], fir_raw.at[c * 2 + half], load_sem.at[8]
            ).start()
    loads[3].start()

    sub8 = lax.broadcasted_iota(jnp.int32, (8, 128), 0)
    lane8 = lax.broadcasted_iota(jnp.int32, (8, 128), 1)
    tile = jnp.zeros((8, 128), jnp.int32)
    for t in range(STEPS):
        for i in range(8):
            tile = jnp.where((sub8 == i) & (lane8 // 64 == t), tok_ref[t, i], tile)
    tokens[w] = tile
    token_send, token_recv = sems.sender(), sems.receiver()

    def token_start(d, carry):
        push(tokens.at[w], tokens.at[w], token_send, token_recv, peer(d))
        return carry

    pl.semaphore_wait(barrier, 65)
    lax.fori_loop(1, 32, token_start, 0)

    lane16 = lax.broadcasted_iota(jnp.int32, (16, 128), 1)
    sub16 = lax.broadcasted_iota(jnp.int32, (16, 128), 0)
    loads[0].wait()

    def gain_rows(k, squares):
        rows = pl.ds(pl.multiple_of(k * 16, 16), 16)
        values = emb[rows, :].astype(F32)
        xg[rows, :] = (values * hyena_gain_ref[...]).astype(BF16)
        return jnp.where(lane16 == k, jnp.sum(values * values, axis=1, keepdims=True), squares)

    sums[0] = lax.fori_loop(0, 32, gain_rows, jnp.zeros((16, 128), F32), unroll=4)
    scales_ready = share_scales(place, sems, sums.at[0], sums_got.at[0], scales.at[0])

    def load_kv(h, carry):
        for j in range(2):
            lanes = pl.ds(pl.multiple_of(h * 128, 128), 128)
            pltpu.make_async_copy(kv_hbm.at[j, :, :, lanes], kv_raw.at[h, j], load_sem.at[6]).start()
        return carry

    loads[1].wait()

    def project(k, carry):
        c, m = k // 2, k % 2
        rows = pl.ds(pl.multiple_of(m * 256, 256), 256)
        table[c, rows, :] = dot(xg[rows, :], hyena_in[c]).astype(BF16)
        return carry

    lax.fori_loop(0, 6, project, 0)
    loads[4].start()
    loads[5].start()
    lax.fori_loop(0, 64, load_kv, 0)

    drain(token_recv, tokens.at[pl.ds(0, 31)])
    drain(token_send, tokens.at[pl.ds(0, 31)])
    vocab = lax.broadcasted_iota(jnp.int32, (64, 512), 1)

    def pick(m):
        rows = tokens[pl.ds(m * 8, 8)].reshape(64, 128)
        for t in range(STEPS):
            hot = (rows[:, t * 64 : t * 64 + 1] == vocab).astype(F32).astype(BF16)
            for c in range(3):
                picked = dot(hot, table[c]).astype(BF16).reshape(4, 16, 256)
                zsend[0, m, t * 4 : t * 4 + 4, :, c * 256 : (c + 1) * 256] = picked

    terms = rs_narrow(place, sems, zsend.at[0], pick, zcore.at[0], ztemp.at[0], zrecv.at[0])
    scales_ready()

    own = tokens[w]
    mine = jnp.concatenate([own[:, 0:1], own[:, 64:65]], axis=0)
    hot16 = (mine == lax.broadcasted_iota(jnp.int32, (16, 512), 1)).astype(F32).astype(BF16)
    hidden0[...] = dot(hot16, emb[...])

    loads[2].wait()
    pltpu.make_async_copy(fir_raw, fir_raw, load_sem.at[8]).wait()
    poles = poles_ref[...][None]
    residues = residues_ref[...][None]

    def filters(g, carry):
        rows = pl.ds(pl.multiple_of(g * 8, 8), 8)
        own_tokens = tokens[n * 8 + g]
        proj = []
        for t in range(STEPS):
            column = own_tokens[:, t * 64 : t * 64 + 1]
            picked = jnp.zeros((8, 128), F32)
            for r in range(16):
                picked = jnp.where(column == lane8 * 16 + r, scales[0, r : r + 1, :], picked)
            scale = jnp.sum(picked, axis=1, keepdims=True)
            got = qkv[pl.ds(pl.multiple_of(t * 64 + g * 8, 8), 8), :] * scale
            proj.append([got[:, c * 256 : (c + 1) * 256] for c in range(3)])
        olds = []
        for slot in range(2):
            old = []
            for c in range(3):
                halves = [fir[c * 2 + half, pl.ds(g * 16 + slot, 8, stride=2), :] for half in range(2)]
                old.append(jnp.concatenate(halves, axis=1))
            olds.append(old)
        taps = [[taps_ref[k, c : c + 1, :] for c in range(3)] for k in range(3)]
        step0 = [taps[0][c] * proj[0][c] + taps[1][c] * olds[0][c] + taps[2][c] * olds[1][c] for c in range(3)]
        step1 = [taps[0][c] * proj[1][c] + taps[1][c] * proj[0][c] + taps[2][c] * olds[0][c] for c in range(3)]
        for slot in range(2):
            for c in range(3):
                for half in range(2):
                    fir[c * 2 + half, pl.ds(g * 16 + slot, 8, stride=2), :] = proj[1 - slot][c][
                        :, half * 128 : half * 128 + 128
                    ]
        state = modal[rows]
        mixer = []
        for step in (step0, step1):
            gated = step[1] * step[2]
            state = poles * state + gated[:, None, :]
            mixed = jnp.sum(residues * state, axis=1) + skip_ref[...] * gated
            mixer.append(step[0] * mixed)
        modal[rows] = state
        mixers[n, g] = jnp.concatenate(mixer, axis=0).astype(BF16)
        return carry

    def sum_terms(k, carry):
        qkv[pl.ds(pl.multiple_of(k * 16, 16), 16), :] = total_of(terms[0][k], terms[1][k], terms[2][k])
        return carry

    lax.fori_loop(0, 8, sum_terms, 0)
    lax.fori_loop(0, 8, filters, 0)
    modal_store = pltpu.make_async_copy(modal, modal_out_hbm, load_sem.at[7])
    modal_store.start()
    for c in range(3):
        for half in range(2):
            pltpu.make_async_copy(
                fir_raw.at[c * 2 + half], fir_out_hbm.at[:, c, :, pl.ds(half * 128, 128)], load_sem.at[8]
            ).start()
    ag_narrow(place, sems, mixers)

    def out_projection(k, rows, weights, sink):
        def fill_a(y):
            block = rows[pl.ds(y * 8, 8)].reshape(128, 256)
            psend[k, 0, pl.ds(y * 8, 8)] = dot(block, weights[:, :HALF]).astype(BF16).reshape(8, 16, HALF)

        def fill_b(x):
            block = jnp.concatenate(
                [rows[(y * 2 + zl) * 4 + x] for zl in range(2) for y in range(4)], axis=0
            )
            psend[k, 1, pl.ds(x * 8, 8)] = dot(block, weights[:, HALF:]).astype(BF16).reshape(8, 16, HALF)

        gens = []
        for p, (axes, fill) in enumerate(((("y", "x"), fill_a), (("x", "y"), fill_b))):
            bufs = [b.at[k, p] for b in (far, close, temp, mid, inbox)]
            sem = rs_sem.at[k, p]
            rs_sems = (sems.sender(), sem.at[pl.ds(0, 4)], sem.at[pl.ds(4, 4)], sem.at[8])
            gens.append(rs_wide_part(place, rs_sems, axes, psend.at[k, p], bufs, fill, sink(p)))
        interleave(*gens)

    loads[3].wait()
    zl, x, y = place.zl, place.x, place.y

    def sink_hidden(p):
        def sink(total):
            cols = pl.ds(p * HALF, HALF)
            hidden1[p] = (hidden0[:, cols] + total).astype(BF16)

        return sink

    out_projection(0, mixers.reshape(32, 16, 256), hyena_out, sink_hidden)
    held[0, (y * 2 + zl) * 4 + x] = hidden1[0]
    held[1, (x * 2 + zl) * 4 + y] = hidden1[1]
    squares = jnp.sum(total_of(hidden1[0]) ** 2 + total_of(hidden1[1]) ** 2, axis=1, keepdims=True)
    sums[1] = jnp.broadcast_to(squares, (16, 128))
    scales_ready = share_scales(place, sems, sums.at[1], sums_got.at[1], scales.at[1])
    gens = []
    for p, axes in enumerate((("y", "x"), ("x", "y"))):
        sem = ag_sem.at[p]
        ag_sems = (sems.sender(), sem.at[pl.ds(0, 8)], sem.at[pl.ds(8, 8)], sem.at[16])
        gens.append(ag_wide_part(place, ag_sems, axes, held.at[p]))
    interleave(*gens)

    loads[4].wait()

    def gather_rows(k, carry):
        a = held[0, k]
        b = held[1, ((k % 4) * 2 + (k // 4) % 2) * 4 + k // 8]
        both = jnp.concatenate([a, b], axis=1).astype(F32)
        rows = pl.ds(pl.multiple_of(k * 16, 16), 16)
        xg[rows, :] = (both * attn_gain_ref[...]).astype(BF16)
        return carry

    lax.fori_loop(0, 32, gather_rows, 0, unroll=4)

    for c in range(3):

        def project_qkv(m, carry):
            rows = pl.ds(pl.multiple_of(m * 256, 256), 256)
            got = dot(xg[rows, :], attn_in[c])
            wide_qkv[2 * c, rows, :] = got[:, :128]
            wide_qkv[2 * c + 1, rows, :] = got[:, 128:]
            return carry

        lax.fori_loop(0, 2, project_qkv, 0)

    def split(m):
        for t in range(2):
            for j in range(2):
                first = (t * 2 + j) * 2
                for c in range(3):
                    for half in range(2):
                        piece = wide_qkv[2 * c + half, pl.ds(t * 8 + m * 2 + j, 32, stride=16), :]
                        lanes = slice(c * 256 + half * 128, c * 256 + half * 128 + 128)
                        zsend[1, m, first : first + 2, :, lanes] = piece.astype(BF16).reshape(2, 16, 128)

    zh, core = place.zh, place.c
    mate = place.narrow(0, 1)
    core_send = sems.sender()
    core_recv = [sems.receiver(), sems.receiver()]
    route_send, route_recv = sems.sender(), sems.receiver()
    for d in (1, 0):
        half = (zh + d) % 2
        split(half * 2 + 1 - core)
        push(zsend.at[1, half * 2 + 1 - core], zcore.at[1, half], core_send, core_recv[d], mate)
    for half in range(2):
        spread[half] = jnp.zeros((512, 128), F32)
        spread[2 + half] = jnp.zeros((512, 128), F32)
    for d in (1, 0):
        across = (zh + d) % 2
        for tj in range(4):
            t, j = tj // 2, tj % 2
            if tj == 0:
                split(across * 2 + core)
                drain(core_recv[d], zcore.at[1, 0])
            rows = slice(tj * 2, tj * 2 + 2)
            total = total_of(zsend[1, across * 2 + core, rows], zcore[1, across, rows]).reshape(32, 768)
            for c in range(3):
                at = j * 8 + (t if c == 0 else 4 + 2 * t + (c - 1))
                for half in range(2):
                    lo = c * 256 + half * 128
                    spread[2 * d + half, pl.ds(at, 32, stride=16), :] = total[:, lo : lo + 128]

        def pack(k, carry):
            rows = pl.ds(pl.multiple_of(k * 16, 16), 16)
            both = jnp.concatenate([spread[2 * d, rows, :], spread[2 * d + 1, rows, :]], axis=1)
            spread16[d, k] = both.astype(BF16)
            return carry

        lax.fori_loop(0, 32, pack, 0, unroll=8)

        def route(k, carry):
            push(
                spread16.at[d, (w + k) % 32],
                routed.at[zh, w],
                route_send,
                route_recv,
                ((w + k) % 32, across * 2 + core),
            )
            return carry

        lax.fori_loop(1 - d, 32, route, 0)
    routed[zh, w] = spread16[0, w]

    kind = sub16 % 8
    late = (kind == 1) | (kind == 6)
    turns = (kind == 0) | (kind == 1) | (kind == 4) | (kind == 6)
    length = jnp.where(sub16 < 8, len_ref[0], len_ref[1])
    place_of = jnp.where(turns, length + jnp.where(late, 1, 0), 0).astype(F32)
    freqs = jnp.exp(-math.log(10000.0) * (lane16 % 64).astype(F32) * 2.0 / HEAD_DIM)
    angles = place_of * freqs
    cos = jnp.cos(angles)
    sin = jnp.where(lane16 < 64, -jnp.sin(angles), jnp.sin(angles))
    lane2 = lax.broadcasted_iota(jnp.int32, (16, 256), 1)
    sub2 = lax.broadcasted_iota(jnp.int32, (16, 256), 0)
    position = (lane2 % 128) // 2
    length2 = jnp.where(sub2 < 8, len_ref[0], len_ref[1])
    valid = (
        (lane2 % 2 == 0)
        & (lane2 // 128 == sub2 // 8)
        & ((position < length2) | (position == 62) | ((position == 63) & (sub2 % 8 == 1)))
    )
    inv = 1.0 / math.sqrt(HEAD_DIM)

    pltpu.make_async_copy(kv_raw, kv_raw, load_sem.at[6]).wait()
    kv = kv_raw.reshape(64, 256, 128)
    routed_all = routed.reshape(64, 16, 256)
    scales_ready()
    row_scale = jnp.zeros((16, 128), F32)
    for t in range(2):
        for j in range(2):
            here = scales[1, pl.ds(t * 8 + n * 2 + j, 1), :]
            own_rows = (sub16 == j * 8 + t) | (sub16 == j * 8 + 4 + 2 * t) | (sub16 == j * 8 + 5 + 2 * t)
            row_scale = jnp.where(own_rows, here, row_scale)
    drain(route_recv, routed_all.at[pl.ds(0, 63)])
    drain(route_send, routed_all.at[pl.ds(0, 63)])
    drain(core_send, zsend.at[1, pl.ds(0, 2)])

    def turn(k, carry):
        for hh in range(2):
            h = k * 2 + hh
            lanes = slice(hh * 128, hh * 128 + 128)
            vectors = total_of(routed[0, k, :, lanes], routed[1, k, :, lanes]) * row_scale
            vectors = vectors.astype(BF16).astype(F32)
            turned = vectors * cos + pltpu.roll(vectors, 64, axis=1) * sin
            turned16[h] = turned.astype(BF16)
            for j in range(2):
                old = kv[h, j * 128 + 112 : j * 128 + 128, :].astype(F32)
                fresh = jnp.where(sub8 >= 4, turned[j * 8 : j * 8 + 8], old[8:16])
                kv[h, j * 128 + 112 : j * 128 + 128, :] = jnp.concatenate([old[0:8], fresh], axis=0).astype(BF16)
        return carry

    lax.fori_loop(0, 32, turn, 0, unroll=4)

    def score(h, carry):
        scored[h] = dot_t(turned16[h], kv[h])
        return carry

    lax.fori_loop(0, 64, score, 0, unroll=8)

    def soften(h, carry):
        score = jnp.where(valid, scored[h] * inv, -1e30)
        grown = jnp.exp(score - jnp.max(score, axis=1, keepdims=True))
        weight = grown / jnp.sum(grown, axis=1, keepdims=True)
        weights16[h] = pltpu.roll(weight, 1, axis=1).astype(BF16)
        return carry

    lax.fori_loop(0, 64, soften, 0, unroll=8)

    def attend(k, carry):
        message = jnp.zeros((8, 128), F32)
        for hh in range(2):
            got = dot(weights16[k * 2 + hh], kv[k * 2 + hh])
            for j in range(2):
                at = hh * 4 + j * 2
                moved = pltpu.roll(got[j * 8 : j * 8 + 8], at, axis=0) if at else got[0:8]
                message = jnp.where((sub8 >= at) & (sub8 < at + 2), moved, message)
        att_send[k] = message.astype(BF16).astype(F32)
        return carry

    lax.fori_loop(0, 32, attend, 0, unroll=4)
    att_out_sem, att_in_sem = sems.sender(), sems.receiver()

    def spread_att(d, carry):
        push(att_send.at[(w + d) % 32], att_recv.at[zh, w], att_out_sem, att_in_sem, peer(d))
        return carry

    lax.fori_loop(1, 64, spread_att, 0)
    att_recv[zh, w] = att_send[w]
    att_all = att_recv.reshape(64, 8, 128)
    drain(att_in_sem, att_all.at[pl.ds(0, 63)])
    flat = att_recv.reshape(512, 128)
    swap_send, swap_recv = sems.sender(), sems.receiver()
    for m in range(2):
        for jt in range(4):
            for hh in range(2):
                piece = flat[pl.ds(m * 256 + hh * 4 + jt, 32, stride=8), :]
                piece = piece.astype(BF16).reshape(2, 16, 128)
                att_rows[m * 2 + core, jt * 2 : jt * 2 + 2, :, hh * 128 : hh * 128 + 128] = piece
        block = att_rows.at[m * 2 + core]
        push(block, block, swap_send, swap_recv, mate)
    drain(swap_recv, att_rows.at[pl.ds(0, 2)])
    drain(swap_send, att_rows.at[pl.ds(0, 2)])
    drain(att_out_sem, att_all.at[pl.ds(0, 63)])
    for m in range(4):
        for jt in range(4):
            j, t = jt // 2, jt % 2
            for hh in range(2):
                piece = att_rows[m, jt * 2 : jt * 2 + 2, :, hh * 128 : hh * 128 + 128].astype(F32)
                spread[hh, pl.ds(t * 8 + m * 2 + j, 32, stride=16), :] = piece.reshape(32, 128)

    def pack_rows(k, carry):
        rows = pl.ds(pl.multiple_of(k * 16, 16), 16)
        both = jnp.concatenate([spread[0, rows, :], spread[1, rows, :]], axis=1)
        att_full[k] = both.astype(BF16)
        return carry

    lax.fori_loop(0, 32, pack_rows, 0, unroll=8)
    loads[5].wait()

    def sink_out(p):
        def sink(total):
            cols = pl.ds(p * HALF, HALF)
            rows = (hidden1[p].astype(F32) + total).astype(BF16)
            out_ref[0, :, cols] = rows[0:8]
            out_ref[1, :, cols] = rows[8:16]

        return sink

    out_projection(1, att_full, attn_out, sink_out)
    modal_store.wait()
    pltpu.make_async_copy(fir_raw, fir_raw, load_sem.at[8]).wait()


def hand_over(a, b, c, out_a, out_b, out_c, held_a, held_b, held_c, sem):
    steps = ((a, held_a, out_a), (b, held_b, out_b), (c, held_c, out_c))
    ins = [pltpu.make_async_copy(src, held, sem.at[k]) for k, (src, held, _) in enumerate(steps)]
    outs = [pltpu.make_async_copy(held, dst, sem.at[3 + k]) for k, (_, held, dst) in enumerate(steps)]
    for copy in ins:
        copy.start()
    for copy_in, copy_out in zip(ins, outs):
        copy_in.wait()
        copy_out.start()
    for copy in outs:
        copy.wait()


def local(
    token_ids,
    lengths,
    embedding,
    hyena_gain,
    hyena_in,
    fir_taps,
    poles,
    residues,
    skip,
    hyena_out,
    modal_state,
    fir_state,
    attn_gain,
    attn_in,
    attn_out,
    kv_cache,
):
    vmem = pl.BlockSpec(memory_space=pltpu.VMEM)
    smem = pl.BlockSpec(memory_space=pltpu.SMEM)
    anywhere = pl.BlockSpec(memory_space=pl.ANY)
    out, modal_out, fir_out = pl.pallas_call(
        kernel,
        out_shape=(
            jax.ShapeDtypeStruct((2, 8, 2048), BF16),
            jax.ShapeDtypeStruct((64, 16, 256), F32),
            jax.ShapeDtypeStruct((64, 3, 2, 256), F32),
        ),
        in_specs=[smem] * 2 + [vmem] * 6 + [anywhere] * 8,
        out_specs=(vmem, anywhere, anywhere),
        scratch_shapes=[
            pltpu.VMEM((512, 2048), BF16),
            pltpu.VMEM((3, 2048, 256), BF16),
            pltpu.VMEM((64, 16, 256), F32),
            pltpu.VMEM((256, 2048), BF16),
            pltpu.VMEM((3, 2048, 256), BF16),
            pltpu.VMEM((256, 2048), BF16),
            pltpu.VMEM((64, 2, 64, 2, 128), BF16),
            pltpu.VMEM((6, 64, 2, 128), F32),
            pltpu.SemaphoreType.DMA((9,)),
            pltpu.SemaphoreType.DMA((16,)),
            pltpu.SemaphoreType.DMA((22,)),
            pltpu.SemaphoreType.DMA((2, 2, 9)),
            pltpu.SemaphoreType.DMA((2, 17)),
            pltpu.VMEM((32, 8, 128), jnp.int32),
            pltpu.VMEM((512, 2048), BF16),
            pltpu.VMEM((3, 512, 256), BF16),
            pltpu.VMEM((2, 4, 8, 16, 768), BF16),
            pltpu.VMEM((2, 2, 8, 16, 768), BF16),
            pltpu.VMEM((2, 8, 16, 768), BF16),
            pltpu.VMEM((2, 8, 16, 768), BF16),
            pltpu.VMEM((2, 16, 128), F32),
            pltpu.VMEM((2, 3, 16, 128), F32),
            pltpu.VMEM((2, 16, 128), F32),
            pltpu.VMEM((4, 8, 16, 256), BF16),
            pltpu.VMEM((2, 2, 32, 16, HALF), BF16),
            pltpu.VMEM((2, 2, 4, 2, 16, HALF), BF16),
            pltpu.VMEM((2, 2, 4, 4, 16, HALF), BF16),
            pltpu.VMEM((2, 2, 4, 2, 16, HALF), BF16),
            pltpu.VMEM((2, 2, 8, 16, HALF), BF16),
            pltpu.VMEM((2, 2, 8, 16, HALF), BF16),
            pltpu.VMEM((16, 2048), F32),
            pltpu.VMEM((2, 16, HALF), BF16),
            pltpu.VMEM((2, 32, 16, HALF), BF16),
            pltpu.VMEM((128, 768), F32),
            pltpu.VMEM((6, 512, 128), F32),
            pltpu.VMEM((4, 512, 128), F32),
            pltpu.VMEM((2, 32, 16, 256), BF16),
            pltpu.VMEM((2, 32, 16, 256), BF16),
            pltpu.VMEM((64, 16, 128), BF16),
            pltpu.VMEM((64, 16, 256), F32),
            pltpu.VMEM((64, 16, 256), BF16),
            pltpu.VMEM((32, 8, 128), F32),
            pltpu.VMEM((2, 32, 8, 128), F32),
            pltpu.VMEM((4, 8, 16, 256), BF16),
            pltpu.VMEM((32, 16, 256), BF16),
        ],
        compiler_params=pltpu.CompilerParams(
            collective_id=0, has_side_effects=True, vmem_limit_bytes=56 * 1024 * 1024
        ),
        name="decode",
    )(
        token_ids,
        lengths,
        hyena_gain[None, :],
        attn_gain[None, :],
        fir_taps,
        poles,
        residues,
        skip[None, :],
        fir_state.transpose(0, 2, 1, 3),
        embedding,
        hyena_in.transpose(1, 0, 2),
        modal_state,
        hyena_out,
        attn_in.transpose(1, 0, 2),
        attn_out,
        kv_cache,
    )
    made = (out, modal_out, fir_out)
    out, modal_out, fir_out = pl.pallas_call(
        hand_over,
        out_shape=[jax.ShapeDtypeStruct(array.shape, array.dtype) for array in made],
        in_specs=[anywhere] * 3,
        out_specs=[anywhere] * 3,
        scratch_shapes=[pltpu.VMEM(array.shape, array.dtype) for array in made]
        + [pltpu.SemaphoreType.DMA((6,))],
        name="hand_over",
    )(*made)
    return out, modal_out, fir_out.transpose(0, 2, 1, 3)


def solution(mesh):
    placed = (
        P(None, "wide"),
        P(("wide", "narrow")),
        P(None, "narrow"),
        P("narrow"),
        P("narrow", None, "wide"),
        P(None, None, "wide"),
        P(None, "wide"),
        P(None, "wide"),
        P("wide"),
        P("wide", "narrow"),
        P("narrow", None, "wide"),
        P("narrow", None, None, "wide"),
        P("narrow"),
        P("narrow", None, "wide"),
        P("wide", "narrow"),
        P(("wide", "narrow"), None, None, None),
    )
    return jax.shard_map(
        local,
        mesh=mesh,
        in_specs=placed,
        out_specs=(
            P(None, "wide", "narrow"),
            P("narrow", None, "wide"),
            P("narrow", None, None, "wide"),
        ),
        check_vma=False,
    )
```

```python
import functools
import math

import jax
import jax.numpy as jnp
from jax import lax
from jax.experimental import pallas as pl
from jax.experimental.pallas import tpu as pltpu
from jax.sharding import PartitionSpec as P

D = 8192
HEADS = 64
HEAD_DIM = 128
STEPS = 2
EPS = 1e-06
MESH = pl.DeviceIdType.MESH
F32 = jnp.float32
BF16 = jnp.bfloat16
HALF = 1024


def dot(a, b):
    return jnp.dot(a, b, preferred_element_type=F32)


def dot_t(a, b):
    return lax.dot_general(a, b, (((1,), (1,)), ((), ())), preferred_element_type=F32)


class Place:
    def __init__(self):
        self.w = lax.axis_index("wide")
        self.n = lax.axis_index("narrow")
        self.y = self.w // 8
        self.zl = (self.w // 4) % 2
        self.x = self.w % 4
        self.zh = self.n // 2
        self.c = self.n % 2

    def along(self, axis, step):
        y = (self.y + step) % 4 if axis == "y" else self.y
        x = (self.x + step) % 4 if axis == "x" else self.x
        zl = (self.zl + step) % 2 if axis == "zl" else self.zl
        return ((y * 2 + zl) * 4 + x, self.n)

    def shifted(self, axis, step, dzl):
        y = (self.y + step) % 4 if axis == "y" else self.y
        x = (self.x + step) % 4 if axis == "x" else self.x
        return ((y * 2 + (self.zl + dzl) % 2) * 4 + x, self.n)

    def narrow(self, dzh, dc):
        return (self.w, ((self.zh + dzh) % 2) * 2 + (self.c + dc) % 2)


class Sems:
    def __init__(self, send, recv):
        self.send, self.recv, self.sends, self.recvs = send, recv, 0, 0

    def sender(self):
        self.sends += 1
        return self.send.at[self.sends - 1]

    def receiver(self):
        self.recvs += 1
        return self.recv.at[self.recvs - 1]


def push(src, dst, send_sem, recv_sem, device):
    pltpu.make_async_remote_copy(
        src_ref=src,
        dst_ref=dst,
        send_sem=send_sem,
        recv_sem=recv_sem,
        device_id=device,
        device_id_type=MESH,
    ).start()


def drain(sem, like):
    pltpu.make_async_copy(like, like, sem).wait()


def total_of(*terms):
    total = terms[0].astype(F32)
    for term in terms[1:]:
        total = total + term.astype(F32)
    return total


def rs_wide_part(place, sems, axes, src, bufs, fill, out):
    far, close, temp, mid, inbox = bufs
    send_sem, far_sem, close_sem, in_sem = sems
    first, second = axes
    f, s = getattr(place, first), getattr(place, second)
    zs = (place.zl, 1 - place.zl)
    steps = (1, 3)

    def block(step, h, o):
        return ((f + step) % 4) * 8 + zs[h] * 4 + (s + o) % 4

    def close_of(h, o):
        return close_sem.at[o if o or not h else 4]

    def hand_on(o):
        drain(far_sem.at[o], far.at[o])
        for h in (1, 0):
            temp[o, h] = total_of(src[block(steps[h], h, o)], far[o, h]).astype(BF16)
            push(temp.at[o, h], close.at[o, h], send_sem, close_of(h, o), place.along(first, steps[h]))

    def send_close(o):
        for h in (1, 0):
            step = steps[1 - h]
            push(src.at[block(step, h, o)], close.at[o, 2 + h], send_sem, close_of(h, o), place.along(first, step))

    def finish(h, o):
        total = total_of(src[block(0, h, o)], close[o, h], close[o, 2 + h])
        if h or o:
            mid[h * 4 + o] = total.astype(BF16)
            there = place.shifted(second, o, h)
            push(mid.at[h * 4 + o], inbox.at[h * 4 + o], send_sem, in_sem, there)
        return total

    fill((f + 2) % 4)
    for o in (2, 1, 3, 0):
        for h in (1, 0):
            push(src.at[block(2, h, o)], far.at[o, h], send_sem, far_sem.at[o], place.along(first, steps[h]))
    yield
    fill((f + 1) % 4)
    fill((f + 3) % 4)
    send_close(2)
    yield
    hand_on(2)
    send_close(1)
    send_close(3)
    yield
    fill(f)
    hand_on(1)
    hand_on(3)
    send_close(0)
    yield
    hand_on(0)
    yield
    for o in (2, 1, 3):
        drain(close_sem.at[o], close.at[o])
        finish(1, o)
        finish(0, o)
        yield
    drain(close_sem.at[4], close.at[0, pl.ds(0, 2)])
    finish(1, 0)
    yield
    drain(close_sem.at[0], close.at[0, pl.ds(0, 2)])
    total = finish(0, 0)
    drain(in_sem, inbox.at[pl.ds(1, 7)])
    for k in range(1, 8):
        total = total + inbox[k].astype(F32)
    out(total)
    drain(send_sem, src.at[pl.ds(0, 31)])


def ag_wide_part(place, sems, axes, held, use):
    first, second = axes
    f, s = getattr(place, first), getattr(place, second)
    zs = (place.zl, 1 - place.zl)
    steps = (1, 3)
    send_sem, in_sem, pass_sem, near_sem, end_sem = sems

    def block(step, h, o):
        return held.at[((f + step) % 4) * 8 + zs[h] * 4 + (s + o) % 4]

    def ring(h, o):
        for d, step in enumerate(steps):
            sem = pass_sem.at[h * 4 + o] if d == h else near_sem
            push(block(0, h, o), block(0, h, o), send_sem, sem, place.along(first, step))

    def line(h):
        for o in (1, 3, 2):
            push(block(0, h, 0), block(0, h, 0), send_sem, in_sem.at[h * 4 + 4 - o], place.shifted(second, o, 0))

    def arrive(h, o):
        drain(in_sem.at[h * 4 + o], block(0, h, o))
        ring(h, o)

    def pass_on(h, o):
        drain(pass_sem.at[h * 4 + o], block(0, h, o))
        got = block(4 - steps[h], h, o)
        push(got, got, send_sem, end_sem, place.along(first, steps[h]))

    push(block(0, 0, 0), block(0, 0, 0), send_sem, in_sem.at[4], place.shifted(second, 0, 1))
    line(0)
    ring(0, 0)
    yield
    drain(in_sem.at[4], block(0, 1, 0))
    line(1)
    ring(1, 0)
    yield
    arrive(0, 1)
    arrive(0, 3)
    yield
    pass_on(0, 0)
    arrive(0, 2)
    yield
    pass_on(1, 0)
    arrive(1, 1)
    arrive(1, 3)
    yield
    arrive(1, 2)
    pass_on(0, 1)
    pass_on(0, 3)
    yield
    use(f)
    yield
    for h, o in ((0, 2), (1, 1), (1, 3), (1, 2)):
        pass_on(h, o)
    yield
    drain(near_sem, held.at[pl.ds(0, 8)])
    use((f + 1) % 4)
    yield
    use((f + 3) % 4)
    yield
    drain(end_sem, held.at[pl.ds(0, 8)])
    use((f + 2) % 4)
    drain(send_sem, held.at[pl.ds(0, 31)])


def interleave(*parts):
    parts = list(parts)
    while parts:
        left = []
        for part in parts:
            try:
                next(part)
                left.append(part)
            except StopIteration:
                pass
        parts = left


def rs_narrow(place, sems, src, fill, core_recv, temp, z_recv):
    zh, c = place.zh, place.c
    mate, across = place.narrow(0, 1), place.narrow(1, 0)
    parts = [pl.ds(p * 4, 4) for p in range(2)]
    send_sem, near_sem = sems.sender(), sems.receiver()
    far_sems = [sems.receiver() for p in parts]
    cross_sems = [sems.receiver() for p in parts]
    over = (1 - zh) * 2 + 1 - c
    fill(over)
    for p, far_sem in zip(parts, far_sems):
        push(src.at[over, p], core_recv.at[0, p], send_sem, far_sem, mate)
    over = (1 - zh) * 2 + c
    fill(over)
    for p, far_sem, cross_sem in zip(parts, far_sems, cross_sems):
        drain(far_sem, temp.at[p])
        temp[p] = total_of(src[over, p], core_recv[0, p]).astype(BF16)
        push(temp.at[p], z_recv.at[p], send_sem, cross_sem, across)
    fill(zh * 2 + 1 - c)
    push(src.at[zh * 2 + 1 - c], core_recv.at[1], send_sem, near_sem, mate)
    fill(zh * 2 + c)
    drain(near_sem, z_recv)
    for p, cross_sem in zip(parts, cross_sems):
        drain(cross_sem, z_recv.at[p])
    drain(send_sem, src.at[pl.ds(0, 3)])
    return [src.at[zh * 2 + c], core_recv.at[1], z_recv]


def share_scales(place, sems, sums, got, scales):
    send_sem, recv_sem = sems.sender(), sems.receiver()
    for k, (dzh, dc) in enumerate(((0, 1), (1, 0), (1, 1))):
        push(sums, got.at[k], send_sem, recv_sem, place.narrow(dzh, dc))

    def finish():
        drain(recv_sem, got)
        drain(send_sem, got)
        total = sums[...] + got[0] + got[1] + got[2]
        scales[...] = lax.rsqrt(total / D + EPS)

    return finish


def kernel(
    tok_ref,
    len_ref,
    hyena_gain_ref,
    attn_gain_ref,
    taps_ref,
    poles_ref,
    residues_ref,
    skip_ref,
    fir_hbm,
    emb_hbm,
    hyena_in_hbm,
    modal_hbm,
    hyena_out_hbm,
    attn_in_hbm,
    attn_out_hbm,
    kv_hbm,
    out_ref,
    modal_out_hbm,
    fir_out_hbm,
    emb,
    hyena_in,
    modal,
    hyena_out,
    attn_in,
    attn_out,
    kv_raw,
    fir_raw,
    load_sem,
    send_sem,
    recv_sem,
    rs_sem,
    ag_sem,
    tokens,
    xg,
    table,
    zsend,
    zcore,
    ztemp,
    zrecv,
    sums,
    sums_got,
    scales,
    mixers,
    psend,
    far,
    close,
    temp,
    mid,
    inbox,
    hidden0,
    hidden1,
    held,
    qkv,
    wide_qkv,
    qkv16,
    route_pick,
    att_pick,
    rsend,
    rcore,
    spread16,
    routed,
    turned16,
    scored,
    weights16,
    att_send,
    att_recv,
    att_rows,
    att_full,
):
    place = Place()
    sems = Sems(send_sem, recv_sem)
    w, n = place.w, place.n

    barrier = pltpu.get_barrier_semaphore()

    def peer(d):
        return ((w + d) % 32, ((place.zh + d // 32) % 2) * 2 + place.c)

    def greet(d, carry):
        pl.semaphore_signal(barrier, inc=1, device_id=peer(d), device_id_type=MESH)
        return carry

    lax.fori_loop(1, 32, greet, 0)
    for dzh, dc in ((0, 1), (1, 0), (1, 1)):
        pl.semaphore_signal(barrier, inc=1, device_id=place.narrow(dzh, dc), device_id_type=MESH)

    loads = []
    for k, (src, dst) in enumerate(
        (
            (emb_hbm, emb),
            (hyena_in_hbm, hyena_in),
            (modal_hbm, modal),
            (hyena_out_hbm, hyena_out),
            (attn_in_hbm, attn_in),
            (attn_out_hbm, attn_out),
        )
    ):
        copy = pltpu.make_async_copy(src, dst, load_sem.at[k])
        loads.append(copy)
    loads[0].start()
    loads[1].start()
    loads[2].start()
    fir = fir_raw.reshape(6, 128, 128)
    for c in range(3):
        for half in range(2):
            pltpu.make_async_copy(
                fir_hbm.at[:, c, :, pl.ds(half * 128, 128)], fir_raw.at[c * 2 + half], load_sem.at[8]
            ).start()
    loads[3].start()

    sub8 = lax.broadcasted_iota(jnp.int32, (8, 128), 0)
    lane8 = lax.broadcasted_iota(jnp.int32, (8, 128), 1)
    tile = jnp.zeros((8, 128), jnp.int32)
    for t in range(STEPS):
        for i in range(8):
            tile = jnp.where((sub8 == i) & (lane8 // 64 == t), tok_ref[t, i], tile)
    tokens[w] = tile
    token_send, token_recv = sems.sender(), sems.receiver()

    def token_start(d, carry):
        push(tokens.at[w], tokens.at[w], token_send, token_recv, peer(d))
        return carry

    pl.semaphore_wait(barrier, 34)
    lax.fori_loop(1, 32, token_start, 0)

    lane16 = lax.broadcasted_iota(jnp.int32, (16, 128), 1)
    sub16 = lax.broadcasted_iota(jnp.int32, (16, 128), 0)
    loads[0].wait()

    def gain_rows(k, squares):
        rows = pl.ds(pl.multiple_of(k * 16, 16), 16)
        values = emb[rows, :].astype(F32)
        xg[rows, :] = (values * hyena_gain_ref[...]).astype(BF16)
        return jnp.where(lane16 == k, jnp.sum(values * values, axis=1, keepdims=True), squares)

    sums[0] = lax.fori_loop(0, 32, gain_rows, jnp.zeros((16, 128), F32), unroll=4)
    scales_ready = share_scales(place, sems, sums.at[0], sums_got.at[0], scales.at[0])

    def load_kv(h, carry):
        for j in range(2):
            lanes = pl.ds(pl.multiple_of(h * 128, 128), 128)
            pltpu.make_async_copy(kv_hbm.at[j, :, :, lanes], kv_raw.at[h, j], load_sem.at[6]).start()
        return carry

    loads[1].wait()

    def project(k, carry):
        c, m = k // 2, k % 2
        rows = pl.ds(pl.multiple_of(m * 256, 256), 256)
        table[c, rows, :] = dot(xg[rows, :], hyena_in[c]).astype(BF16)
        return carry

    lax.fori_loop(0, 6, project, 0)
    loads[4].start()
    loads[5].start()
    lax.fori_loop(0, 64, load_kv, 0)

    drain(token_recv, tokens.at[pl.ds(0, 31)])
    drain(token_send, tokens.at[pl.ds(0, 31)])
    vocab = lax.broadcasted_iota(jnp.int32, (128, 512), 1)

    def pick(m):
        rows = tokens[pl.ds(m * 8, 8)].reshape(64, 128)
        column = jnp.concatenate([rows[:, 0:1], rows[:, 64:65]], axis=0)
        hot = (column == vocab).astype(F32).astype(BF16)
        for c in range(3):
            picked = dot(hot, table[c]).astype(BF16).reshape(8, 16, 256)
            zsend[m, :, :, c * 256 : (c + 1) * 256] = picked

    terms = rs_narrow(place, sems, zsend, pick, zcore, ztemp, zrecv)
    scales_ready()

    own = tokens[w]
    mine = jnp.concatenate([own[:, 0:1], own[:, 64:65]], axis=0)
    hot16 = (mine == lax.broadcasted_iota(jnp.int32, (16, 512), 1)).astype(F32).astype(BF16)
    hidden0[...] = dot(hot16, emb[...])

    loads[2].wait()
    pltpu.make_async_copy(fir_raw, fir_raw, load_sem.at[8]).wait()
    poles = poles_ref[...][None]
    residues = residues_ref[...][None]

    def filters(g, carry):
        rows = pl.ds(pl.multiple_of(g * 8, 8), 8)
        own_tokens = tokens[n * 8 + g]
        proj = []
        for t in range(STEPS):
            column = own_tokens[:, t * 64 : t * 64 + 1]
            picked = jnp.zeros((8, 128), F32)
            for r in range(16):
                picked = jnp.where(column == lane8 * 16 + r, scales[0, r : r + 1, :], picked)
            scale = jnp.sum(picked, axis=1, keepdims=True)
            got = qkv[pl.ds(pl.multiple_of(t * 64 + g * 8, 8), 8), :] * scale
            proj.append([got[:, c * 256 : (c + 1) * 256] for c in range(3)])
        olds = []
        for slot in range(2):
            old = []
            for c in range(3):
                halves = [fir[c * 2 + half, pl.ds(g * 16 + slot, 8, stride=2), :] for half in range(2)]
                old.append(jnp.concatenate(halves, axis=1))
            olds.append(old)
        taps = [[taps_ref[k, c : c + 1, :] for c in range(3)] for k in range(3)]
        step0 = [taps[0][c] * proj[0][c] + taps[1][c] * olds[0][c] + taps[2][c] * olds[1][c] for c in range(3)]
        step1 = [taps[0][c] * proj[1][c] + taps[1][c] * proj[0][c] + taps[2][c] * olds[0][c] for c in range(3)]
        for slot in range(2):
            for c in range(3):
                for half in range(2):
                    fir[c * 2 + half, pl.ds(g * 16 + slot, 8, stride=2), :] = proj[1 - slot][c][
                        :, half * 128 : half * 128 + 128
                    ]
        state = modal[rows]
        mixer = []
        for step in (step0, step1):
            gated = step[1] * step[2]
            state = poles * state + gated[:, None, :]
            mixed = jnp.sum(residues * state, axis=1) + skip_ref[...] * gated
            mixer.append(step[0] * mixed)
        modal[rows] = state
        mixers[n, g] = jnp.concatenate(mixer, axis=0).astype(BF16)
        return carry

    def sum_terms(k, carry):
        qkv[pl.ds(pl.multiple_of(k * 16, 16), 16), :] = total_of(terms[0][k], terms[1][k], terms[2][k])
        return carry

    lax.fori_loop(0, 8, sum_terms, 0)
    mixer_send, mixer_recv = sems.sender(), sems.receiver()
    for part in range(2):
        lax.fori_loop(part * 4, part * 4 + 4, filters, 0, unroll=2)
        done = mixers.at[n, pl.ds(part * 4, 4)]
        for dzh, dc in ((1, 0), (1, 1), (0, 1)):
            push(done, done, mixer_send, mixer_recv, place.narrow(dzh, dc))
    modal_store = pltpu.make_async_copy(modal, modal_out_hbm, load_sem.at[7])
    modal_store.start()
    for c in range(3):
        for half in range(2):
            pltpu.make_async_copy(
                fir_raw.at[c * 2 + half], fir_out_hbm.at[:, c, :, pl.ds(half * 128, 128)], load_sem.at[8]
            ).start()

    to_row = lax.broadcasted_iota(jnp.int32, (128, 384), 0)
    from_row = lax.broadcasted_iota(jnp.int32, (128, 384), 1)
    place_in = to_row % 8
    branch = jnp.where(place_in < 2, 0, jnp.where(place_in < 4, 3, 1 + place_in % 2))
    when = jnp.where(place_in < 2, place_in, (place_in - 4) // 2)
    seen = (to_row // 16 == (from_row % 128) // 16) & (branch == from_row // 128)
    for m in range(4):
        hit = seen & (from_row % 16 == when * 8 + m * 2 + (to_row % 16) // 8)
        route_pick[m] = jnp.where(hit, 1.0, 0.0).astype(BF16)
    to_row = lax.broadcasted_iota(jnp.int32, (128, 256), 0)
    from_row = lax.broadcasted_iota(jnp.int32, (128, 256), 1)
    row = (from_row % 2) * 8 + (from_row // 64) * 2 + (from_row % 4) // 2
    for hh in range(2):
        hit = (to_row // 16 == (from_row % 64) // 8) & ((from_row % 8) // 4 == hh) & (to_row % 16 == row)
        att_pick[hh] = jnp.where(hit, 1.0, 0.0).astype(BF16)
    drain(mixer_recv, mixers.at[pl.ds(0, 3)])
    drain(mixer_send, mixers.at[pl.ds(0, 3)])

    def out_projection(k, rows, weights, sink):
        def fill_a(y):
            block = rows[pl.ds(y * 8, 8)].reshape(128, 256)
            psend[k, 0, pl.ds(y * 8, 8)] = dot(block, weights[:, :HALF]).astype(BF16).reshape(8, 16, HALF)

        def fill_b(x):
            block = jnp.concatenate(
                [rows[(y * 2 + zl) * 4 + x] for zl in range(2) for y in range(4)], axis=0
            )
            psend[k, 1, pl.ds(x * 8, 8)] = dot(block, weights[:, HALF:]).astype(BF16).reshape(8, 16, HALF)

        gens = []
        for p, (axes, fill) in enumerate(((("y", "x"), fill_a), (("x", "y"), fill_b))):
            bufs = [b.at[k, p] for b in (far, close, temp, mid, inbox)]
            sem = rs_sem.at[k, p]
            rs_sems = (sems.sender(), sem.at[pl.ds(0, 4)], sem.at[pl.ds(4, 5)], sem.at[9])
            gens.append(rs_wide_part(place, rs_sems, axes, psend.at[k, p], bufs, fill, sink(p)))
        interleave(*gens)

    loads[3].wait()
    zl, x, y = place.zl, place.x, place.y

    def sink_hidden(p):
        def sink(total):
            cols = pl.ds(p * HALF, HALF)
            hidden1[p] = (hidden0[:, cols] + total).astype(BF16)

        return sink

    out_projection(0, mixers.reshape(32, 16, 256), hyena_out, sink_hidden)
    held[0, (y * 2 + zl) * 4 + x] = hidden1[0]
    held[1, (x * 2 + zl) * 4 + y] = hidden1[1]
    squares = jnp.sum(total_of(hidden1[0]) ** 2 + total_of(hidden1[1]) ** 2, axis=1, keepdims=True)
    sums[1] = jnp.broadcast_to(squares, (16, 128))
    scales_ready = share_scales(place, sems, sums.at[1], sums_got.at[1], scales.at[1])
    loads[4].wait()

    def use_plane(p, plane):
        gain = attn_gain_ref[:, p * HALF : (p + 1) * HALF]
        rows = held[p, pl.ds(plane * 8, 8)].reshape(128, HALF).astype(F32) * gain
        rows = rows.astype(BF16)
        for c in range(3):
            got = dot(rows, attn_in[c, p * HALF : (p + 1) * HALF, :])
            if p == 0:
                wide_qkv[0, c, pl.ds(pl.multiple_of(plane * 128, 128), 128), :] = got
            else:
                for k in range(8):
                    at = pl.multiple_of(((k % 4) * 8 + (k // 4) * 4 + plane) * 16, 16)
                    wide_qkv[1, c, pl.ds(at, 16), :] = got[k * 16 : k * 16 + 16]

    gens = []
    for p, axes in enumerate((("y", "x"), ("x", "y"))):
        sem = ag_sem.at[p]
        ag_sems = (sems.sender(), sem.at[pl.ds(0, 8)], sem.at[pl.ds(8, 8)], sem.at[16], sem.at[17])
        gens.append(ag_wide_part(place, ag_sems, axes, held.at[p], functools.partial(use_plane, p)))
    interleave(*gens)

    def join(k, carry):
        rows = pl.ds(pl.multiple_of(k * 32, 32), 32)
        for c in range(3):
            both = wide_qkv[0, c, rows, :] + wide_qkv[1, c, rows, :]
            qkv16[k // 4, pl.ds(pl.multiple_of(c * 128 + (k % 4) * 32, 32), 32), :] = both.astype(BF16)
        return carry

    lax.fori_loop(0, 16, join, 0, unroll=2)

    def split(m):
        for g in range(4):
            got = dot(route_pick[m], qkv16[g])
            rsend[m, g * 8 : g * 8 + 8] = got.astype(BF16).reshape(8, 16, 256)

    zh, core = place.zh, place.c
    mate = place.narrow(0, 1)
    core_send = sems.sender()
    core_recv = [sems.receiver(), sems.receiver()]
    route_send, route_recv = sems.sender(), sems.receiver()
    for d in (1, 0):
        half = (zh + d) % 2
        split(half * 2 + 1 - core)
        push(rsend.at[half * 2 + 1 - core], rcore.at[half], core_send, core_recv[d], mate)
    split((1 - zh) * 2 + core)
    for d in (1, 0):
        across = (zh + d) % 2
        drain(core_recv[d], rcore.at[0])

        def pack(k, carry):
            spread16[d, k] = total_of(rsend[across * 2 + core, k], rcore[across, k]).astype(BF16)
            return carry

        lax.fori_loop(0, 32, pack, 0, unroll=8)

        def route(k, carry):
            push(
                spread16.at[d, (w + k) % 32],
                routed.at[zh, w],
                route_send,
                route_recv,
                ((w + k) % 32, across * 2 + core),
            )
            return carry

        lax.fori_loop(1 - d, 32, route, 0)
        if d:
            split(zh * 2 + core)
    routed[zh, w] = spread16[0, w]

    kind = sub16 % 8
    late = (kind == 1) | (kind == 6)
    turns = (kind == 0) | (kind == 1) | (kind == 4) | (kind == 6)
    length = jnp.where(sub16 < 8, len_ref[0], len_ref[1])
    place_of = jnp.where(turns, length + jnp.where(late, 1, 0), 0).astype(F32)
    freqs = jnp.exp(-math.log(10000.0) * (lane16 % 64).astype(F32) * 2.0 / HEAD_DIM)
    angles = place_of * freqs
    cos = jnp.cos(angles)
    sin = jnp.where(lane16 < 64, -jnp.sin(angles), jnp.sin(angles))
    lane2 = lax.broadcasted_iota(jnp.int32, (16, 256), 1)
    sub2 = lax.broadcasted_iota(jnp.int32, (16, 256), 0)
    position = (lane2 % 128) // 2
    length2 = jnp.where(sub2 < 8, len_ref[0], len_ref[1])
    valid = (
        (lane2 % 2 == 0)
        & (lane2 // 128 == sub2 // 8)
        & ((position < length2) | (position == 62) | ((position == 63) & (sub2 % 8 == 1)))
    )
    inv = 1.0 / math.sqrt(HEAD_DIM)

    pltpu.make_async_copy(kv_raw, kv_raw, load_sem.at[6]).wait()
    kv = kv_raw.reshape(64, 256, 128)
    routed_all = routed.reshape(64, 16, 256)
    scales_ready()
    row_scale = jnp.zeros((16, 128), F32)
    for t in range(2):
        for j in range(2):
            here = scales[1, pl.ds(t * 8 + n * 2 + j, 1), :]
            own_rows = (sub16 == j * 8 + t) | (sub16 == j * 8 + 4 + 2 * t) | (sub16 == j * 8 + 5 + 2 * t)
            row_scale = jnp.where(own_rows, here, row_scale)
    drain(route_recv, routed_all.at[pl.ds(0, 63)])
    drain(route_send, routed_all.at[pl.ds(0, 63)])
    drain(core_send, rcore)

    def turn(k, carry):
        for hh in range(2):
            h = k * 2 + hh
            lanes = slice(hh * 128, hh * 128 + 128)
            vectors = total_of(routed[0, k, :, lanes], routed[1, k, :, lanes]) * row_scale
            vectors = vectors.astype(BF16).astype(F32)
            turned = vectors * cos + pltpu.roll(vectors, 64, axis=1) * sin
            turned16[h] = turned.astype(BF16)
            for j in range(2):
                old = kv[h, j * 128 + 112 : j * 128 + 128, :].astype(F32)
                fresh = jnp.where(sub8 >= 4, turned[j * 8 : j * 8 + 8], old[8:16])
                kv[h, j * 128 + 112 : j * 128 + 128, :] = jnp.concatenate([old[0:8], fresh], axis=0).astype(BF16)
        return carry

    lax.fori_loop(0, 32, turn, 0, unroll=4)

    def score(h, carry):
        scored[h] = dot_t(turned16[h], kv[h])
        return carry

    lax.fori_loop(0, 64, score, 0, unroll=8)

    def soften(h, carry):
        score = jnp.where(valid, scored[h] * inv, -1e30)
        grown = jnp.exp(score - jnp.max(score, axis=1, keepdims=True))
        weight = grown * (1.0 / jnp.sum(grown, axis=1, keepdims=True))
        weights16[h] = pltpu.roll(weight, 1, axis=1).astype(BF16)
        return carry

    lax.fori_loop(0, 64, soften, 0, unroll=8)

    def attend(k, carry):
        message = jnp.zeros((8, 128), F32)
        for hh in range(2):
            got = dot(weights16[k * 2 + hh], kv[k * 2 + hh])
            for j in range(2):
                at = hh * 4 + j * 2
                moved = pltpu.roll(got[j * 8 : j * 8 + 8], at, axis=0) if at else got[0:8]
                message = jnp.where((sub8 >= at) & (sub8 < at + 2), moved, message)
        att_send[k] = message.astype(BF16).astype(F32)
        return carry

    lax.fori_loop(0, 32, attend, 0, unroll=4)
    att_out_sem, att_in_sem = sems.sender(), sems.receiver()

    def spread_att(d, carry):
        push(att_send.at[(w + d) % 32], att_recv.at[zh, w], att_out_sem, att_in_sem, peer(d))
        return carry

    lax.fori_loop(1, 64, spread_att, 0)
    att_recv[zh, w] = att_send[w]
    att_all = att_recv.reshape(64, 8, 128)
    drain(att_in_sem, att_all.at[pl.ds(0, 63)])
    swap_send, swap_recv = sems.sender(), sems.receiver()
    for m in range(2):

        def take(k, carry):
            pair = att_recv[m, pl.ds(k * 2, 2)].reshape(16, 128)
            att_rows[m * 2 + core, k] = pair.astype(BF16)
            return carry

        lax.fori_loop(0, 16, take, 0, unroll=8)
        block = att_rows.at[m * 2 + core]
        push(block, block, swap_send, swap_recv, mate)
    drain(swap_recv, att_rows.at[pl.ds(0, 2)])
    drain(swap_send, att_rows.at[pl.ds(0, 2)])
    drain(att_out_sem, att_all.at[pl.ds(0, 63)])
    for g in range(4):
        stack = jnp.concatenate([att_rows[m, g * 4 : g * 4 + 4].reshape(64, 128) for m in range(4)], axis=0)
        got = jnp.concatenate([dot(att_pick[hh], stack) for hh in range(2)], axis=1)
        att_full[g * 8 : g * 8 + 8] = got.astype(BF16).reshape(8, 16, 256)
    loads[5].wait()

    def sink_out(p):
        def sink(total):
            cols = pl.ds(p * HALF, HALF)
            rows = (hidden1[p].astype(F32) + total).astype(BF16)
            out_ref[0, :, cols] = rows[0:8]
            out_ref[1, :, cols] = rows[8:16]

        return sink

    out_projection(1, att_full, attn_out, sink_out)
    modal_store.wait()
    pltpu.make_async_copy(fir_raw, fir_raw, load_sem.at[8]).wait()


def hand_over(a, b, c, out_a, out_b, out_c, held_a, held_b, held_c, sem):
    steps = ((a, held_a, out_a), (b, held_b, out_b), (c, held_c, out_c))
    ins = [pltpu.make_async_copy(src, held, sem.at[k]) for k, (src, held, _) in enumerate(steps)]
    outs = [pltpu.make_async_copy(held, dst, sem.at[3 + k]) for k, (_, held, dst) in enumerate(steps)]
    for copy in ins:
        copy.start()
    for copy_in, copy_out in zip(ins, outs):
        copy_in.wait()
        copy_out.start()
    for copy in outs:
        copy.wait()


def local(
    token_ids,
    lengths,
    embedding,
    hyena_gain,
    hyena_in,
    fir_taps,
    poles,
    residues,
    skip,
    hyena_out,
    modal_state,
    fir_state,
    attn_gain,
    attn_in,
    attn_out,
    kv_cache,
):
    vmem = pl.BlockSpec(memory_space=pltpu.VMEM)
    smem = pl.BlockSpec(memory_space=pltpu.SMEM)
    anywhere = pl.BlockSpec(memory_space=pl.ANY)
    out, modal_out, fir_out = pl.pallas_call(
        kernel,
        out_shape=(
            jax.ShapeDtypeStruct((2, 8, 2048), BF16),
            jax.ShapeDtypeStruct((64, 16, 256), F32),
            jax.ShapeDtypeStruct((64, 3, 2, 256), F32),
        ),
        in_specs=[smem] * 2 + [vmem] * 6 + [anywhere] * 8,
        out_specs=(vmem, anywhere, anywhere),
        scratch_shapes=[
            pltpu.VMEM((512, 2048), BF16),
            pltpu.VMEM((3, 2048, 256), BF16),
            pltpu.VMEM((64, 16, 256), F32),
            pltpu.VMEM((256, 2048), BF16),
            pltpu.VMEM((3, 2048, 256), BF16),
            pltpu.VMEM((256, 2048), BF16),
            pltpu.VMEM((64, 2, 64, 2, 128), BF16),
            pltpu.VMEM((6, 64, 2, 128), F32),
            pltpu.SemaphoreType.DMA((9,)),
            pltpu.SemaphoreType.DMA((16,)),
            pltpu.SemaphoreType.DMA((22,)),
            pltpu.SemaphoreType.DMA((2, 2, 10)),
            pltpu.SemaphoreType.DMA((2, 18)),
            pltpu.VMEM((32, 8, 128), jnp.int32),
            pltpu.VMEM((512, 2048), BF16),
            pltpu.VMEM((3, 512, 256), BF16),
            pltpu.VMEM((4, 8, 16, 768), BF16),
            pltpu.VMEM((2, 8, 16, 768), BF16),
            pltpu.VMEM((8, 16, 768), BF16),
            pltpu.VMEM((8, 16, 768), BF16),
            pltpu.VMEM((2, 16, 128), F32),
            pltpu.VMEM((2, 3, 16, 128), F32),
            pltpu.VMEM((2, 16, 128), F32),
            pltpu.VMEM((4, 8, 16, 256), BF16),
            pltpu.VMEM((2, 2, 32, 16, HALF), BF16),
            pltpu.VMEM((2, 2, 4, 2, 16, HALF), BF16),
            pltpu.VMEM((2, 2, 4, 4, 16, HALF), BF16),
            pltpu.VMEM((2, 2, 4, 2, 16, HALF), BF16),
            pltpu.VMEM((2, 2, 8, 16, HALF), BF16),
            pltpu.VMEM((2, 2, 8, 16, HALF), BF16),
            pltpu.VMEM((16, 2048), F32),
            pltpu.VMEM((2, 16, HALF), BF16),
            pltpu.VMEM((2, 32, 16, HALF), BF16),
            pltpu.VMEM((128, 768), F32),
            pltpu.VMEM((2, 3, 512, 256), F32),
            pltpu.VMEM((4, 384, 256), BF16),
            pltpu.VMEM((4, 128, 384), BF16),
            pltpu.VMEM((2, 128, 256), BF16),
            pltpu.VMEM((4, 32, 16, 256), BF16),
            pltpu.VMEM((2, 32, 16, 256), BF16),
            pltpu.VMEM((2, 32, 16, 256), BF16),
            pltpu.VMEM((2, 32, 16, 256), BF16),
            pltpu.VMEM((64, 16, 128), BF16),
            pltpu.VMEM((64, 16, 256), F32),
            pltpu.VMEM((64, 16, 256), BF16),
            pltpu.VMEM((32, 8, 128), F32),
            pltpu.VMEM((2, 32, 8, 128), F32),
            pltpu.VMEM((4, 16, 16, 128), BF16),
            pltpu.VMEM((32, 16, 256), BF16),
        ],
        compiler_params=pltpu.CompilerParams(
            collective_id=0, has_side_effects=True, vmem_limit_bytes=56 * 1024 * 1024
        ),
        name="decode",
    )(
        token_ids,
        lengths,
        hyena_gain[None, :],
        attn_gain[None, :],
        fir_taps,
        poles,
        residues,
        skip[None, :],
        fir_state.transpose(0, 2, 1, 3),
        embedding,
        hyena_in.transpose(1, 0, 2),
        modal_state,
        hyena_out,
        attn_in.transpose(1, 0, 2),
        attn_out,
        kv_cache,
    )
    made = (out, modal_out, fir_out)
    out, modal_out, fir_out = pl.pallas_call(
        hand_over,
        out_shape=[jax.ShapeDtypeStruct(array.shape, array.dtype) for array in made],
        in_specs=[anywhere] * 3,
        out_specs=[anywhere] * 3,
        scratch_shapes=[pltpu.VMEM(array.shape, array.dtype) for array in made]
        + [pltpu.SemaphoreType.DMA((6,))],
        name="hand_over",
    )(*made)
    return out, modal_out, fir_out.transpose(0, 2, 1, 3)


def solution(mesh):
    placed = (
        P(None, "wide"),
        P(("wide", "narrow")),
        P(None, "narrow"),
        P("narrow"),
        P("narrow", None, "wide"),
        P(None, None, "wide"),
        P(None, "wide"),
        P(None, "wide"),
        P("wide"),
        P("wide", "narrow"),
        P("narrow", None, "wide"),
        P("narrow", None, None, "wide"),
        P("narrow"),
        P("narrow", None, "wide"),
        P("wide", "narrow"),
        P(("wide", "narrow"), None, None, None),
    )
    return jax.shard_map(
        local,
        mesh=mesh,
        in_specs=placed,
        out_specs=(
            P(None, "wide", "narrow"),
            P("narrow", None, "wide"),
            P("narrow", None, None, "wide"),
        ),
        check_vma=False,
    )
```

```python
import functools
import math

import jax
import jax.numpy as jnp
from jax import lax
from jax.experimental import pallas as pl
from jax.experimental.pallas import tpu as pltpu
from jax.sharding import PartitionSpec as P

D = 8192
HEADS = 64
HEAD_DIM = 128
STEPS = 2
EPS = 1e-06
MESH = pl.DeviceIdType.MESH
F32 = jnp.float32
BF16 = jnp.bfloat16
HALF = 1024


def dot(a, b):
    return jnp.dot(a, b, preferred_element_type=F32)


def dot_t(a, b):
    return lax.dot_general(a, b, (((1,), (1,)), ((), ())), preferred_element_type=F32)


class Place:
    def __init__(self):
        self.w = lax.axis_index("wide")
        self.n = lax.axis_index("narrow")
        self.y = self.w // 8
        self.zl = (self.w // 4) % 2
        self.x = self.w % 4
        self.zh = self.n // 2
        self.c = self.n % 2

    def along(self, axis, step):
        y = (self.y + step) % 4 if axis == "y" else self.y
        x = (self.x + step) % 4 if axis == "x" else self.x
        zl = (self.zl + step) % 2 if axis == "zl" else self.zl
        return ((y * 2 + zl) * 4 + x, self.n)

    def shifted(self, axis, step, dzl):
        y = (self.y + step) % 4 if axis == "y" else self.y
        x = (self.x + step) % 4 if axis == "x" else self.x
        return ((y * 2 + (self.zl + dzl) % 2) * 4 + x, self.n)

    def narrow(self, dzh, dc):
        return (self.w, ((self.zh + dzh) % 2) * 2 + (self.c + dc) % 2)


class Sems:
    def __init__(self, send, recv):
        self.send, self.recv, self.sends, self.recvs = send, recv, 0, 0

    def sender(self):
        self.sends += 1
        return self.send.at[self.sends - 1]

    def receiver(self):
        self.recvs += 1
        return self.recv.at[self.recvs - 1]


def push(src, dst, send_sem, recv_sem, device):
    pltpu.make_async_remote_copy(
        src_ref=src,
        dst_ref=dst,
        send_sem=send_sem,
        recv_sem=recv_sem,
        device_id=device,
        device_id_type=MESH,
    ).start()


def drain(sem, like):
    pltpu.make_async_copy(like, like, sem).wait()


def total_of(*terms):
    total = terms[0].astype(F32)
    for term in terms[1:]:
        total = total + term.astype(F32)
    return total


def rs_wide_part(place, sems, axes, src, bufs, fill, out):
    far, close, temp, mid, inbox, over = bufs
    send_sem, far_sem, close_sem, in_sem, over_sem = sems
    first, second = axes
    f, s = getattr(place, first), getattr(place, second)
    zs = (place.zl, 1 - place.zl)
    steps = (1, 3)

    def block(step, h, o):
        return ((f + step) % 4) * 8 + zs[h] * 4 + (s + o) % 4

    def cross(step):
        fill((f + step) % 4)
        push(src.at[block(step, 1, 0)], over.at[step], send_sem, over_sem.at[step], place.along("zl", 1))

    def crossed(step):
        drain(over_sem.at[step], over.at[step])
        return total_of(src[block(step, 0, 0)], over[step])

    def hand_on(o):
        drain(far_sem.at[o], far.at[o])
        for h in (1, 0):
            temp[o, h] = total_of(src[block(steps[h], h, o)], far[o, h]).astype(BF16)
            push(temp.at[o, h], close.at[o, h], send_sem, close_sem.at[o], place.along(first, steps[h]))

    def send_close(o):
        for h in (1, 0):
            step = steps[1 - h]
            push(src.at[block(step, h, o)], close.at[o, 2 + h], send_sem, close_sem.at[o], place.along(first, step))

    cross(2)
    for o in (2, 1, 3):
        for h in (1, 0):
            push(src.at[block(2, h, o)], far.at[o, h], send_sem, far_sem.at[o], place.along(first, steps[h]))
    yield
    cross(1)
    cross(3)
    send_close(2)
    yield
    hand_on(2)
    send_close(1)
    send_close(3)
    yield
    temp[0, 0] = crossed(2).astype(BF16)
    push(temp.at[0, 0], far.at[0, 0], send_sem, far_sem.at[0], place.along(first, 1))
    yield
    cross(0)
    yield
    hand_on(1)
    hand_on(3)
    yield
    temp[0, 1] = crossed(3).astype(BF16)
    push(temp.at[0, 1], close.at[0, 2], send_sem, close_sem.at[0], place.along(first, 3))
    yield
    for o in (2, 1, 3):
        if o == 2:
            drain(far_sem.at[0], far.at[0, 0])
            mid[0] = (crossed(1) + far[0, 0].astype(F32)).astype(BF16)
            push(mid.at[0], close.at[0, 0], send_sem, close_sem.at[0], place.along(first, 1))
            yield
        drain(close_sem.at[o], close.at[o])
        for h in (1, 0):
            total = total_of(src[block(0, h, o)], close[o, h], close[o, 2 + h])
            mid[h * 4 + o] = total.astype(BF16)
            there = place.shifted(second, o, h)
            push(mid.at[h * 4 + o], inbox.at[h * 4 + o], send_sem, in_sem, there)
        yield
    total = crossed(0)
    drain(close_sem.at[0], close.at[0, pl.ds(0, 2)])
    total = total + close[0, 0].astype(F32) + close[0, 2].astype(F32)
    yield
    drain(in_sem, inbox.at[pl.ds(0, 6)])
    for h in range(2):
        for o in (1, 2, 3):
            total = total + inbox[h * 4 + o].astype(F32)
    out(total)
    drain(send_sem, src.at[pl.ds(0, 31)])


def ag_wide_part(place, sems, axes, held, use):
    first, second = axes
    f, s = getattr(place, first), getattr(place, second)
    zs = (place.zl, 1 - place.zl)
    steps = (1, 3)
    send_sem, in_sem, pass_sem, near_sem, end_sem = sems

    def block(step, h, o):
        return held.at[((f + step) % 4) * 8 + zs[h] * 4 + (s + o) % 4]

    def ring(h, o):
        for d, step in enumerate(steps):
            sem = pass_sem.at[h * 4 + o] if d == h else near_sem
            push(block(0, h, o), block(0, h, o), send_sem, sem, place.along(first, step))

    def line(h):
        for o in (1, 3, 2):
            push(block(0, h, 0), block(0, h, 0), send_sem, in_sem.at[h * 4 + 4 - o], place.shifted(second, o, 0))

    def arrive(h, o):
        drain(in_sem.at[h * 4 + o], block(0, h, o))
        ring(h, o)

    def pass_on(h, o):
        drain(pass_sem.at[h * 4 + o], block(0, h, o))
        got = block(4 - steps[h], h, o)
        push(got, got, send_sem, end_sem, place.along(first, steps[h]))

    push(block(0, 0, 0), block(0, 0, 0), send_sem, in_sem.at[4], place.shifted(second, 0, 1))
    line(0)
    ring(0, 0)
    yield
    drain(in_sem.at[4], block(0, 1, 0))
    line(1)
    ring(1, 0)
    yield
    arrive(0, 1)
    arrive(0, 3)
    yield
    pass_on(0, 0)
    arrive(0, 2)
    yield
    pass_on(1, 0)
    arrive(1, 1)
    arrive(1, 3)
    yield
    arrive(1, 2)
    pass_on(0, 1)
    pass_on(0, 3)
    yield
    use(f)
    yield
    for h, o in ((0, 2), (1, 1), (1, 3), (1, 2)):
        pass_on(h, o)
    yield
    drain(near_sem, held.at[pl.ds(0, 8)])
    use((f + 1) % 4)
    yield
    use((f + 3) % 4)
    yield
    drain(end_sem, held.at[pl.ds(0, 8)])
    use((f + 2) % 4)
    drain(send_sem, held.at[pl.ds(0, 31)])


def interleave(*parts):
    parts = list(parts)
    while parts:
        left = []
        for part in parts:
            try:
                next(part)
                left.append(part)
            except StopIteration:
                pass
        parts = left


def rs_narrow(place, sems, src, fill, core_recv, temp, z_recv):
    zh, c = place.zh, place.c
    mate, across = place.narrow(0, 1), place.narrow(1, 0)
    parts = [pl.ds(p * 4, 4) for p in range(2)]
    send_sem, near_sem = sems.sender(), sems.receiver()
    far_sems = [sems.receiver() for p in parts]
    cross_sems = [sems.receiver() for p in parts]
    over = (1 - zh) * 2 + 1 - c
    fill(over)
    for p, far_sem in zip(parts, far_sems):
        push(src.at[over, p], core_recv.at[0, p], send_sem, far_sem, mate)
    over = (1 - zh) * 2 + c
    fill(over)
    for p, far_sem, cross_sem in zip(parts, far_sems, cross_sems):
        drain(far_sem, temp.at[p])
        temp[p] = total_of(src[over, p], core_recv[0, p]).astype(BF16)
        push(temp.at[p], z_recv.at[p], send_sem, cross_sem, across)
    fill(zh * 2 + 1 - c)
    push(src.at[zh * 2 + 1 - c], core_recv.at[1], send_sem, near_sem, mate)
    fill(zh * 2 + c)
    drain(near_sem, z_recv)
    for p, cross_sem in zip(parts, cross_sems):
        drain(cross_sem, z_recv.at[p])
    drain(send_sem, src.at[pl.ds(0, 3)])
    return [src.at[zh * 2 + c], core_recv.at[1], z_recv]


def share_scales(place, sems, sums, got, scales):
    send_sem, recv_sem = sems.sender(), sems.receiver()
    for k, (dzh, dc) in enumerate(((0, 1), (1, 0), (1, 1))):
        push(sums, got.at[k], send_sem, recv_sem, place.narrow(dzh, dc))

    def finish():
        drain(recv_sem, got)
        drain(send_sem, got)
        total = sums[...] + got[0] + got[1] + got[2]
        scales[...] = lax.rsqrt(total / D + EPS)

    return finish


def kernel(
    tok_ref,
    len_ref,
    hyena_gain_ref,
    attn_gain_ref,
    taps_ref,
    poles_ref,
    residues_ref,
    skip_ref,
    fir_hbm,
    emb_hbm,
    hyena_in_hbm,
    modal_hbm,
    hyena_out_hbm,
    attn_in_hbm,
    attn_out_hbm,
    kv_hbm,
    out_ref,
    modal_out_hbm,
    fir_out_hbm,
    emb,
    hyena_in,
    modal,
    hyena_out,
    attn_in,
    attn_out,
    kv_raw,
    fir_raw,
    load_sem,
    send_sem,
    recv_sem,
    rs_sem,
    ag_sem,
    tokens,
    xg,
    table,
    zsend,
    zcore,
    ztemp,
    zrecv,
    sums,
    sums_got,
    scales,
    mixers,
    psend,
    far,
    close,
    temp,
    mid,
    inbox,
    over,
    hidden0,
    hidden1,
    held,
    qkv,
    wide_qkv,
    qkv16,
    route_pick,
    att_pick,
    rsend,
    rcore,
    spread16,
    routed,
    turned16,
    scored,
    weights16,
    att_send,
    att_recv,
    att_rows,
    att_full,
):
    place = Place()
    sems = Sems(send_sem, recv_sem)
    w, n = place.w, place.n

    barrier = pltpu.get_barrier_semaphore()

    def peer(d):
        return ((w + d) % 32, ((place.zh + d // 32) % 2) * 2 + place.c)

    def greet(d, carry):
        pl.semaphore_signal(barrier, inc=1, device_id=peer(d), device_id_type=MESH)
        return carry

    lax.fori_loop(1, 32, greet, 0)
    for dzh, dc in ((0, 1), (1, 0), (1, 1)):
        pl.semaphore_signal(barrier, inc=1, device_id=place.narrow(dzh, dc), device_id_type=MESH)

    loads = []
    for k, (src, dst) in enumerate(
        (
            (emb_hbm, emb),
            (hyena_in_hbm, hyena_in),
            (modal_hbm, modal),
            (hyena_out_hbm, hyena_out),
            (attn_in_hbm, attn_in),
            (attn_out_hbm, attn_out),
        )
    ):
        copy = pltpu.make_async_copy(src, dst, load_sem.at[k])
        loads.append(copy)
    loads[0].start()
    loads[1].start()
    loads[2].start()
    fir = fir_raw.reshape(6, 128, 128)
    for c in range(3):
        for half in range(2):
            pltpu.make_async_copy(
                fir_hbm.at[:, c, :, pl.ds(half * 128, 128)], fir_raw.at[c * 2 + half], load_sem.at[8]
            ).start()
    loads[3].start()

    sub8 = lax.broadcasted_iota(jnp.int32, (8, 128), 0)
    lane8 = lax.broadcasted_iota(jnp.int32, (8, 128), 1)
    tile = jnp.zeros((8, 128), jnp.int32)
    for t in range(STEPS):
        for i in range(8):
            tile = jnp.where((sub8 == i) & (lane8 // 64 == t), tok_ref[t, i], tile)
    tokens[w] = tile
    token_send, token_recv = sems.sender(), sems.receiver()

    def token_start(d, carry):
        push(tokens.at[w], tokens.at[w], token_send, token_recv, peer(d))
        return carry

    pl.semaphore_wait(barrier, 34)
    lax.fori_loop(1, 32, token_start, 0)

    lane16 = lax.broadcasted_iota(jnp.int32, (16, 128), 1)
    sub16 = lax.broadcasted_iota(jnp.int32, (16, 128), 0)
    loads[0].wait()

    def gain_rows(k, squares):
        rows = pl.ds(pl.multiple_of(k * 16, 16), 16)
        values = emb[rows, :].astype(F32)
        xg[rows, :] = (values * hyena_gain_ref[...]).astype(BF16)
        return jnp.where(lane16 == k, jnp.sum(values * values, axis=1, keepdims=True), squares)

    sums[0] = lax.fori_loop(0, 32, gain_rows, jnp.zeros((16, 128), F32), unroll=4)
    scales_ready = share_scales(place, sems, sums.at[0], sums_got.at[0], scales.at[0])

    def load_kv(h, carry):
        for j in range(2):
            lanes = pl.ds(pl.multiple_of(h * 128, 128), 128)
            pltpu.make_async_copy(kv_hbm.at[j, :, :, lanes], kv_raw.at[h, j], load_sem.at[6]).start()
        return carry

    loads[1].wait()

    def project(k, carry):
        c, m = k // 2, k % 2
        rows = pl.ds(pl.multiple_of(m * 256, 256), 256)
        table[c, rows, :] = dot(xg[rows, :], hyena_in[c]).astype(BF16)
        return carry

    lax.fori_loop(0, 6, project, 0)
    loads[4].start()
    loads[5].start()
    lax.fori_loop(0, 64, load_kv, 0)

    drain(token_recv, tokens.at[pl.ds(0, 31)])
    drain(token_send, tokens.at[pl.ds(0, 31)])
    vocab = lax.broadcasted_iota(jnp.int32, (128, 512), 1)

    def pick(m):
        rows = tokens[pl.ds(m * 8, 8)].reshape(64, 128)
        column = jnp.concatenate([rows[:, 0:1], rows[:, 64:65]], axis=0)
        hot = (column == vocab).astype(F32).astype(BF16)
        for c in range(3):
            picked = dot(hot, table[c]).astype(BF16).reshape(8, 16, 256)
            zsend[m, :, :, c * 256 : (c + 1) * 256] = picked

    terms = rs_narrow(place, sems, zsend, pick, zcore, ztemp, zrecv)
    scales_ready()

    own = tokens[w]
    mine = jnp.concatenate([own[:, 0:1], own[:, 64:65]], axis=0)
    hot16 = (mine == lax.broadcasted_iota(jnp.int32, (16, 512), 1)).astype(F32).astype(BF16)
    hidden0[...] = dot(hot16, emb[...])

    loads[2].wait()
    pltpu.make_async_copy(fir_raw, fir_raw, load_sem.at[8]).wait()
    poles = poles_ref[...][None]
    residues = residues_ref[...][None]

    def filters(g, carry):
        rows = pl.ds(pl.multiple_of(g * 8, 8), 8)
        own_tokens = tokens[n * 8 + g]
        proj = []
        for t in range(STEPS):
            column = own_tokens[:, t * 64 : t * 64 + 1]
            picked = jnp.zeros((8, 128), F32)
            for r in range(16):
                picked = jnp.where(column == lane8 * 16 + r, scales[0, r : r + 1, :], picked)
            scale = jnp.sum(picked, axis=1, keepdims=True)
            got = qkv[pl.ds(pl.multiple_of(t * 64 + g * 8, 8), 8), :] * scale
            proj.append([got[:, c * 256 : (c + 1) * 256] for c in range(3)])
        olds = []
        for slot in range(2):
            old = []
            for c in range(3):
                halves = [fir[c * 2 + half, pl.ds(g * 16 + slot, 8, stride=2), :] for half in range(2)]
                old.append(jnp.concatenate(halves, axis=1))
            olds.append(old)
        taps = [[taps_ref[k, c : c + 1, :] for c in range(3)] for k in range(3)]
        step0 = [taps[0][c] * proj[0][c] + taps[1][c] * olds[0][c] + taps[2][c] * olds[1][c] for c in range(3)]
        step1 = [taps[0][c] * proj[1][c] + taps[1][c] * proj[0][c] + taps[2][c] * olds[0][c] for c in range(3)]
        for slot in range(2):
            for c in range(3):
                for half in range(2):
                    fir[c * 2 + half, pl.ds(g * 16 + slot, 8, stride=2), :] = proj[1 - slot][c][
                        :, half * 128 : half * 128 + 128
                    ]
        state = modal[rows]
        mixer = []
        for step in (step0, step1):
            gated = step[1] * step[2]
            state = poles * state + gated[:, None, :]
            mixed = jnp.sum(residues * state, axis=1) + skip_ref[...] * gated
            mixer.append(step[0] * mixed)
        modal[rows] = state
        mixers[n, g] = jnp.concatenate(mixer, axis=0).astype(BF16)
        return carry

    def sum_terms(k, carry):
        qkv[pl.ds(pl.multiple_of(k * 16, 16), 16), :] = total_of(terms[0][k], terms[1][k], terms[2][k])
        return carry

    lax.fori_loop(0, 8, sum_terms, 0)
    mixer_send, mixer_recv = sems.sender(), sems.receiver()
    for part in range(2):
        lax.fori_loop(part * 4, part * 4 + 4, filters, 0, unroll=4)
        done = mixers.at[n, pl.ds(part * 4, 4)]
        for dzh, dc in ((1, 0), (1, 1), (0, 1)):
            push(done, done, mixer_send, mixer_recv, place.narrow(dzh, dc))
    modal_store = pltpu.make_async_copy(modal, modal_out_hbm, load_sem.at[7])
    modal_store.start()
    for c in range(3):
        for half in range(2):
            pltpu.make_async_copy(
                fir_raw.at[c * 2 + half], fir_out_hbm.at[:, c, :, pl.ds(half * 128, 128)], load_sem.at[8]
            ).start()

    to_row = lax.broadcasted_iota(jnp.int32, (128, 384), 0)
    from_row = lax.broadcasted_iota(jnp.int32, (128, 384), 1)
    place_in = to_row % 8
    branch = jnp.where(place_in < 2, 0, jnp.where(place_in < 4, 3, 1 + place_in % 2))
    when = jnp.where(place_in < 2, place_in, (place_in - 4) // 2)
    seen = (to_row // 16 == (from_row % 128) // 16) & (branch == from_row // 128)
    for m in range(4):
        hit = seen & (from_row % 16 == when * 8 + m * 2 + (to_row % 16) // 8)
        route_pick[m] = jnp.where(hit, 1.0, 0.0).astype(BF16)
    to_row = lax.broadcasted_iota(jnp.int32, (128, 256), 0)
    from_row = lax.broadcasted_iota(jnp.int32, (128, 256), 1)
    row = (from_row % 2) * 8 + (from_row // 64) * 2 + (from_row % 4) // 2
    for hh in range(2):
        hit = (to_row // 16 == (from_row % 64) // 8) & ((from_row % 8) // 4 == hh) & (to_row % 16 == row)
        att_pick[hh] = jnp.where(hit, 1.0, 0.0).astype(BF16)
    drain(mixer_recv, mixers.at[pl.ds(0, 3)])
    drain(mixer_send, mixers.at[pl.ds(0, 3)])

    def out_projection(k, rows, weights, sink):
        def fill_a(y):
            block = rows[pl.ds(y * 8, 8)].reshape(128, 256)
            psend[k, 0, pl.ds(y * 8, 8)] = dot(block, weights[:, :HALF]).astype(BF16).reshape(8, 16, HALF)

        def fill_b(x):
            block = jnp.concatenate(
                [rows[(y * 2 + zl) * 4 + x] for zl in range(2) for y in range(4)], axis=0
            )
            psend[k, 1, pl.ds(x * 8, 8)] = dot(block, weights[:, HALF:]).astype(BF16).reshape(8, 16, HALF)

        gens = []
        for p, (axes, fill) in enumerate(((("y", "x"), fill_a), (("x", "y"), fill_b))):
            bufs = [b.at[k, p] for b in (far, close, temp, mid, inbox, over)]
            sem = rs_sem.at[k, p]
            rs_sems = (sems.sender(), sem.at[pl.ds(0, 4)], sem.at[pl.ds(4, 4)], sem.at[8], sem.at[pl.ds(9, 4)])
            gens.append(rs_wide_part(place, rs_sems, axes, psend.at[k, p], bufs, fill, sink(p)))
        interleave(*gens)

    loads[3].wait()
    zl, x, y = place.zl, place.x, place.y

    def sink_hidden(p):
        def sink(total):
            cols = pl.ds(p * HALF, HALF)
            hidden1[p] = (hidden0[:, cols] + total).astype(BF16)

        return sink

    out_projection(0, mixers.reshape(32, 16, 256), hyena_out, sink_hidden)
    held[0, (y * 2 + zl) * 4 + x] = hidden1[0]
    held[1, (x * 2 + zl) * 4 + y] = hidden1[1]
    squares = jnp.sum(total_of(hidden1[0]) ** 2 + total_of(hidden1[1]) ** 2, axis=1, keepdims=True)
    sums[1] = jnp.broadcast_to(squares, (16, 128))
    scales_ready = share_scales(place, sems, sums.at[1], sums_got.at[1], scales.at[1])
    loads[4].wait()

    def use_plane(p, plane):
        gain = attn_gain_ref[:, p * HALF : (p + 1) * HALF]
        rows = held[p, pl.ds(plane * 8, 8)].reshape(128, HALF).astype(F32) * gain
        rows = rows.astype(BF16)
        for c in range(3):
            got = dot(rows, attn_in[c, p * HALF : (p + 1) * HALF, :])
            if p == 0:
                wide_qkv[0, c, pl.ds(pl.multiple_of(plane * 128, 128), 128), :] = got
            else:
                for k in range(8):
                    at = pl.multiple_of(((k % 4) * 8 + (k // 4) * 4 + plane) * 16, 16)
                    wide_qkv[1, c, pl.ds(at, 16), :] = got[k * 16 : k * 16 + 16]

    gens = []
    for p, axes in enumerate((("y", "x"), ("x", "y"))):
        sem = ag_sem.at[p]
        ag_sems = (sems.sender(), sem.at[pl.ds(0, 8)], sem.at[pl.ds(8, 8)], sem.at[16], sem.at[17])
        gens.append(ag_wide_part(place, ag_sems, axes, held.at[p], functools.partial(use_plane, p)))
    interleave(*gens)

    def join(k, carry):
        rows = pl.ds(pl.multiple_of(k * 32, 32), 32)
        for c in range(3):
            both = wide_qkv[0, c, rows, :] + wide_qkv[1, c, rows, :]
            qkv16[k // 4, pl.ds(pl.multiple_of(c * 128 + (k % 4) * 32, 32), 32), :] = both.astype(BF16)
        return carry

    lax.fori_loop(0, 16, join, 0, unroll=2)

    def split(m):
        for g in range(4):
            got = dot(route_pick[m], qkv16[g])
            rsend[m, g * 8 : g * 8 + 8] = got.astype(BF16).reshape(8, 16, 256)

    zh, core = place.zh, place.c
    mate = place.narrow(0, 1)
    core_send = sems.sender()
    core_recv = [sems.receiver(), sems.receiver()]
    route_send, route_recv = sems.sender(), sems.receiver()
    for d in (1, 0):
        half = (zh + d) % 2
        split(half * 2 + 1 - core)
        push(rsend.at[half * 2 + 1 - core], rcore.at[half], core_send, core_recv[d], mate)
    split((1 - zh) * 2 + core)
    for d in (1, 0):
        across = (zh + d) % 2
        drain(core_recv[d], rcore.at[0])

        def pack(k, carry):
            spread16[d, k] = total_of(rsend[across * 2 + core, k], rcore[across, k]).astype(BF16)
            return carry

        lax.fori_loop(0, 32, pack, 0, unroll=8)

        def route(k, carry):
            push(
                spread16.at[d, (w + k) % 32],
                routed.at[zh, w],
                route_send,
                route_recv,
                ((w + k) % 32, across * 2 + core),
            )
            return carry

        lax.fori_loop(1 - d, 32, route, 0)
        if d:
            split(zh * 2 + core)
    routed[zh, w] = spread16[0, w]

    kind = sub16 % 8
    late = (kind == 1) | (kind == 6)
    turns = (kind == 0) | (kind == 1) | (kind == 4) | (kind == 6)
    length = jnp.where(sub16 < 8, len_ref[0], len_ref[1])
    place_of = jnp.where(turns, length + jnp.where(late, 1, 0), 0).astype(F32)
    freqs = jnp.exp(-math.log(10000.0) * (lane16 % 64).astype(F32) * 2.0 / HEAD_DIM)
    angles = place_of * freqs
    cos = jnp.cos(angles)
    sin = jnp.where(lane16 < 64, -jnp.sin(angles), jnp.sin(angles))
    lane2 = lax.broadcasted_iota(jnp.int32, (16, 256), 1)
    sub2 = lax.broadcasted_iota(jnp.int32, (16, 256), 0)
    position = (lane2 % 128) // 2
    length2 = jnp.where(sub2 < 8, len_ref[0], len_ref[1])
    valid = (
        (lane2 % 2 == 0)
        & (lane2 // 128 == sub2 // 8)
        & ((position < length2) | (position == 62) | ((position == 63) & (sub2 % 8 == 1)))
    )
    inv = 1.0 / math.sqrt(HEAD_DIM)

    pltpu.make_async_copy(kv_raw, kv_raw, load_sem.at[6]).wait()
    kv = kv_raw.reshape(64, 256, 128)
    routed_all = routed.reshape(64, 16, 256)
    scales_ready()
    row_scale = jnp.zeros((16, 128), F32)
    for t in range(2):
        for j in range(2):
            here = scales[1, pl.ds(t * 8 + n * 2 + j, 1), :]
            own_rows = (sub16 == j * 8 + t) | (sub16 == j * 8 + 4 + 2 * t) | (sub16 == j * 8 + 5 + 2 * t)
            row_scale = jnp.where(own_rows, here, row_scale)
    drain(route_recv, routed_all.at[pl.ds(0, 63)])
    drain(route_send, routed_all.at[pl.ds(0, 63)])
    drain(core_send, rcore)

    def turn(k, carry):
        for hh in range(2):
            h = k * 2 + hh
            lanes = slice(hh * 128, hh * 128 + 128)
            vectors = total_of(routed[0, k, :, lanes], routed[1, k, :, lanes]) * row_scale
            vectors = vectors.astype(BF16).astype(F32)
            turned = vectors * cos + pltpu.roll(vectors, 64, axis=1) * sin
            turned16[h] = turned.astype(BF16)
            for j in range(2):
                old = kv[h, j * 128 + 112 : j * 128 + 128, :].astype(F32)
                fresh = jnp.where(sub8 >= 4, turned[j * 8 : j * 8 + 8], old[8:16])
                kv[h, j * 128 + 112 : j * 128 + 128, :] = jnp.concatenate([old[0:8], fresh], axis=0).astype(BF16)
        return carry

    lax.fori_loop(0, 32, turn, 0, unroll=4)

    def score(h, carry):
        scored[h] = dot_t(turned16[h], kv[h])
        return carry

    lax.fori_loop(0, 64, score, 0, unroll=8)

    def soften(h, carry):
        score = jnp.where(valid, scored[h] * inv, -1e30)
        grown = jnp.exp(score - jnp.max(score, axis=1, keepdims=True))
        weight = grown * (1.0 / jnp.sum(grown, axis=1, keepdims=True))
        weights16[h] = pltpu.roll(weight, 1, axis=1).astype(BF16)
        return carry

    lax.fori_loop(0, 64, soften, 0, unroll=8)

    def attend(k, carry):
        message = jnp.zeros((8, 128), F32)
        for hh in range(2):
            got = dot(weights16[k * 2 + hh], kv[k * 2 + hh])
            for j in range(2):
                at = hh * 4 + j * 2
                moved = pltpu.roll(got[j * 8 : j * 8 + 8], at, axis=0) if at else got[0:8]
                message = jnp.where((sub8 >= at) & (sub8 < at + 2), moved, message)
        att_send[k] = message.astype(BF16).astype(F32)
        return carry

    lax.fori_loop(0, 32, attend, 0, unroll=4)
    att_out_sem, att_in_sem = sems.sender(), sems.receiver()

    def spread_att(d, carry):
        push(att_send.at[(w + d) % 32], att_recv.at[zh, w], att_out_sem, att_in_sem, peer(d))
        return carry

    lax.fori_loop(1, 64, spread_att, 0)
    att_recv[zh, w] = att_send[w]
    att_all = att_recv.reshape(64, 8, 128)
    drain(att_in_sem, att_all.at[pl.ds(0, 63)])
    swap_send, swap_recv = sems.sender(), sems.receiver()
    for m in range(2):

        def take(k, carry):
            pair = att_recv[m, pl.ds(k * 2, 2)].reshape(16, 128)
            att_rows[m * 2 + core, k] = pair.astype(BF16)
            return carry

        lax.fori_loop(0, 16, take, 0, unroll=8)
        block = att_rows.at[m * 2 + core]
        push(block, block, swap_send, swap_recv, mate)
    drain(swap_recv, att_rows.at[pl.ds(0, 2)])
    drain(swap_send, att_rows.at[pl.ds(0, 2)])
    drain(att_out_sem, att_all.at[pl.ds(0, 63)])
    for g in range(4):
        stack = jnp.concatenate([att_rows[m, g * 4 : g * 4 + 4].reshape(64, 128) for m in range(4)], axis=0)
        got = jnp.concatenate([dot(att_pick[hh], stack) for hh in range(2)], axis=1)
        att_full[g * 8 : g * 8 + 8] = got.astype(BF16).reshape(8, 16, 256)
    loads[5].wait()

    def sink_out(p):
        def sink(total):
            cols = pl.ds(p * HALF, HALF)
            rows = (hidden1[p].astype(F32) + total).astype(BF16)
            out_ref[0, :, cols] = rows[0:8]
            out_ref[1, :, cols] = rows[8:16]

        return sink

    out_projection(1, att_full, attn_out, sink_out)
    modal_store.wait()
    pltpu.make_async_copy(fir_raw, fir_raw, load_sem.at[8]).wait()


def hand_over(a, b, c, out_a, out_b, out_c, held_a, held_b, held_c, sem):
    steps = ((a, held_a, out_a), (b, held_b, out_b), (c, held_c, out_c))
    ins = [pltpu.make_async_copy(src, held, sem.at[k]) for k, (src, held, _) in enumerate(steps)]
    outs = [pltpu.make_async_copy(held, dst, sem.at[3 + k]) for k, (_, held, dst) in enumerate(steps)]
    for copy in ins:
        copy.start()
    for copy_in, copy_out in zip(ins, outs):
        copy_in.wait()
        copy_out.start()
    for copy in outs:
        copy.wait()


def local(
    token_ids,
    lengths,
    embedding,
    hyena_gain,
    hyena_in,
    fir_taps,
    poles,
    residues,
    skip,
    hyena_out,
    modal_state,
    fir_state,
    attn_gain,
    attn_in,
    attn_out,
    kv_cache,
):
    vmem = pl.BlockSpec(memory_space=pltpu.VMEM)
    smem = pl.BlockSpec(memory_space=pltpu.SMEM)
    anywhere = pl.BlockSpec(memory_space=pl.ANY)
    out, modal_out, fir_out = pl.pallas_call(
        kernel,
        out_shape=(
            jax.ShapeDtypeStruct((2, 8, 2048), BF16),
            jax.ShapeDtypeStruct((64, 16, 256), F32),
            jax.ShapeDtypeStruct((64, 3, 2, 256), F32),
        ),
        in_specs=[smem] * 2 + [vmem] * 6 + [anywhere] * 8,
        out_specs=(vmem, anywhere, anywhere),
        scratch_shapes=[
            pltpu.VMEM((512, 2048), BF16),
            pltpu.VMEM((3, 2048, 256), BF16),
            pltpu.VMEM((64, 16, 256), F32),
            pltpu.VMEM((256, 2048), BF16),
            pltpu.VMEM((3, 2048, 256), BF16),
            pltpu.VMEM((256, 2048), BF16),
            pltpu.VMEM((64, 2, 64, 2, 128), BF16),
            pltpu.VMEM((6, 64, 2, 128), F32),
            pltpu.SemaphoreType.DMA((9,)),
            pltpu.SemaphoreType.DMA((16,)),
            pltpu.SemaphoreType.DMA((22,)),
            pltpu.SemaphoreType.DMA((2, 2, 13)),
            pltpu.SemaphoreType.DMA((2, 18)),
            pltpu.VMEM((32, 8, 128), jnp.int32),
            pltpu.VMEM((512, 2048), BF16),
            pltpu.VMEM((3, 512, 256), BF16),
            pltpu.VMEM((4, 8, 16, 768), BF16),
            pltpu.VMEM((2, 8, 16, 768), BF16),
            pltpu.VMEM((8, 16, 768), BF16),
            pltpu.VMEM((8, 16, 768), BF16),
            pltpu.VMEM((2, 16, 128), F32),
            pltpu.VMEM((2, 3, 16, 128), F32),
            pltpu.VMEM((2, 16, 128), F32),
            pltpu.VMEM((4, 8, 16, 256), BF16),
            pltpu.VMEM((2, 2, 32, 16, HALF), BF16),
            pltpu.VMEM((2, 2, 4, 2, 16, HALF), BF16),
            pltpu.VMEM((2, 2, 4, 4, 16, HALF), BF16),
            pltpu.VMEM((2, 2, 4, 2, 16, HALF), BF16),
            pltpu.VMEM((2, 2, 8, 16, HALF), BF16),
            pltpu.VMEM((2, 2, 8, 16, HALF), BF16),
            pltpu.VMEM((2, 2, 4, 16, HALF), BF16),
            pltpu.VMEM((16, 2048), F32),
            pltpu.VMEM((2, 16, HALF), BF16),
            pltpu.VMEM((2, 32, 16, HALF), BF16),
            pltpu.VMEM((128, 768), F32),
            pltpu.VMEM((2, 3, 512, 256), F32),
            pltpu.VMEM((4, 384, 256), BF16),
            pltpu.VMEM((4, 128, 384), BF16),
            pltpu.VMEM((2, 128, 256), BF16),
            pltpu.VMEM((4, 32, 16, 256), BF16),
            pltpu.VMEM((2, 32, 16, 256), BF16),
            pltpu.VMEM((2, 32, 16, 256), BF16),
            pltpu.VMEM((2, 32, 16, 256), BF16),
            pltpu.VMEM((64, 16, 128), BF16),
            pltpu.VMEM((64, 16, 256), F32),
            pltpu.VMEM((64, 16, 256), BF16),
            pltpu.VMEM((32, 8, 128), F32),
            pltpu.VMEM((2, 32, 8, 128), F32),
            pltpu.VMEM((4, 16, 16, 128), BF16),
            pltpu.VMEM((32, 16, 256), BF16),
        ],
        compiler_params=pltpu.CompilerParams(
            collective_id=0, has_side_effects=True, vmem_limit_bytes=56 * 1024 * 1024
        ),
        name="decode",
    )(
        token_ids,
        lengths,
        hyena_gain[None, :],
        attn_gain[None, :],
        fir_taps,
        poles,
        residues,
        skip[None, :],
        fir_state.transpose(0, 2, 1, 3),
        embedding,
        hyena_in.transpose(1, 0, 2),
        modal_state,
        hyena_out,
        attn_in.transpose(1, 0, 2),
        attn_out,
        kv_cache,
    )
    made = (out, modal_out, fir_out)
    out, modal_out, fir_out = pl.pallas_call(
        hand_over,
        out_shape=[jax.ShapeDtypeStruct(array.shape, array.dtype) for array in made],
        in_specs=[anywhere] * 3,
        out_specs=[anywhere] * 3,
        scratch_shapes=[pltpu.VMEM(array.shape, array.dtype) for array in made]
        + [pltpu.SemaphoreType.DMA((6,))],
        name="hand_over",
    )(*made)
    return out, modal_out, fir_out.transpose(0, 2, 1, 3)


def solution(mesh):
    placed = (
        P(None, "wide"),
        P(("wide", "narrow")),
        P(None, "narrow"),
        P("narrow"),
        P("narrow", None, "wide"),
        P(None, None, "wide"),
        P(None, "wide"),
        P(None, "wide"),
        P("wide"),
        P("wide", "narrow"),
        P("narrow", None, "wide"),
        P("narrow", None, None, "wide"),
        P("narrow"),
        P("narrow", None, "wide"),
        P("wide", "narrow"),
        P(("wide", "narrow"), None, None, None),
    )
    return jax.shard_map(
        local,
        mesh=mesh,
        in_specs=placed,
        out_specs=(
            P(None, "wide", "narrow"),
            P("narrow", None, "wide"),
            P("narrow", None, None, "wide"),
        ),
        check_vma=False,
    )
```

```python
import functools
import math

import jax
import jax.numpy as jnp
from jax import lax
from jax.experimental import pallas as pl
from jax.experimental.pallas import tpu as pltpu
from jax.sharding import PartitionSpec as P

D = 8192
HEADS = 64
HEAD_DIM = 128
STEPS = 2
EPS = 1e-06
MESH = pl.DeviceIdType.MESH
F32 = jnp.float32
BF16 = jnp.bfloat16
HALF = 1024


def dot(a, b):
    return jnp.dot(a, b, preferred_element_type=F32)


def dot_t(a, b):
    return lax.dot_general(a, b, (((1,), (1,)), ((), ())), preferred_element_type=F32)


class Place:
    def __init__(self):
        self.w = lax.axis_index("wide")
        self.n = lax.axis_index("narrow")
        self.y = self.w // 8
        self.zl = (self.w // 4) % 2
        self.x = self.w % 4
        self.zh = self.n // 2
        self.c = self.n % 2

    def along(self, axis, step):
        y = (self.y + step) % 4 if axis == "y" else self.y
        x = (self.x + step) % 4 if axis == "x" else self.x
        zl = (self.zl + step) % 2 if axis == "zl" else self.zl
        return ((y * 2 + zl) * 4 + x, self.n)

    def shifted(self, axis, step, dzl):
        y = (self.y + step) % 4 if axis == "y" else self.y
        x = (self.x + step) % 4 if axis == "x" else self.x
        return ((y * 2 + (self.zl + dzl) % 2) * 4 + x, self.n)

    def narrow(self, dzh, dc):
        return (self.w, ((self.zh + dzh) % 2) * 2 + (self.c + dc) % 2)


class Sems:
    def __init__(self, send, recv):
        self.send, self.recv, self.sends, self.recvs = send, recv, 0, 0

    def sender(self):
        self.sends += 1
        return self.send.at[self.sends - 1]

    def receiver(self):
        self.recvs += 1
        return self.recv.at[self.recvs - 1]


def push(src, dst, send_sem, recv_sem, device):
    pltpu.make_async_remote_copy(
        src_ref=src,
        dst_ref=dst,
        send_sem=send_sem,
        recv_sem=recv_sem,
        device_id=device,
        device_id_type=MESH,
    ).start()


def drain(sem, like):
    pltpu.make_async_copy(like, like, sem).wait()


def total_of(*terms):
    total = terms[0].astype(F32)
    for term in terms[1:]:
        total = total + term.astype(F32)
    return total


def rs_wide_part(place, sems, axes, src, bufs, fill, out):
    far, close, temp, mid, inbox, over = bufs
    send_sem, far_sem, close_sem, in_sem, over_sem = sems
    first, second = axes
    f, s = getattr(place, first), getattr(place, second)
    zs = (place.zl, 1 - place.zl)
    steps = (1, 3)

    def block(step, h, o):
        return ((f + step) % 4) * 8 + zs[h] * 4 + (s + o) % 4

    def cross(step):
        fill((f + step) % 4)
        push(src.at[block(step, 1, 0)], over.at[step], send_sem, over_sem.at[step], place.along("zl", 1))

    def crossed(step):
        drain(over_sem.at[step], over.at[step])
        return total_of(src[block(step, 0, 0)], over[step])

    def hand_on(o):
        drain(far_sem.at[o], far.at[o])
        for h in (1, 0):
            temp[o, h] = total_of(src[block(steps[h], h, o)], far[o, h]).astype(BF16)
            push(temp.at[o, h], close.at[o, h], send_sem, close_sem.at[o], place.along(first, steps[h]))

    def send_close(o):
        for h in (1, 0):
            step = steps[1 - h]
            push(src.at[block(step, h, o)], close.at[o, 2 + h], send_sem, close_sem.at[o], place.along(first, step))

    cross(2)
    for o in (2, 1, 3):
        for h in (1, 0):
            push(src.at[block(2, h, o)], far.at[o, h], send_sem, far_sem.at[o], place.along(first, steps[h]))
    yield
    cross(1)
    cross(3)
    send_close(2)
    yield
    hand_on(2)
    send_close(1)
    send_close(3)
    yield
    temp[0, 0] = crossed(2).astype(BF16)
    push(temp.at[0, 0], far.at[0, 0], send_sem, far_sem.at[0], place.along(first, 1))
    yield
    cross(0)
    yield
    hand_on(1)
    hand_on(3)
    yield
    temp[0, 1] = crossed(3).astype(BF16)
    push(temp.at[0, 1], close.at[0, 2], send_sem, close_sem.at[0], place.along(first, 3))
    yield
    for o in (2, 1, 3):
        if o == 2:
            drain(far_sem.at[0], far.at[0, 0])
            mid[0] = (crossed(1) + far[0, 0].astype(F32)).astype(BF16)
            push(mid.at[0], close.at[0, 0], send_sem, close_sem.at[0], place.along(first, 1))
            yield
        drain(close_sem.at[o], close.at[o])
        for h in (1, 0):
            total = total_of(src[block(0, h, o)], close[o, h], close[o, 2 + h])
            mid[h * 4 + o] = total.astype(BF16)
            there = place.shifted(second, o, h)
            push(mid.at[h * 4 + o], inbox.at[h * 4 + o], send_sem, in_sem, there)
        yield
    total = crossed(0)
    drain(close_sem.at[0], close.at[0, pl.ds(0, 2)])
    total = total + close[0, 0].astype(F32) + close[0, 2].astype(F32)
    yield
    drain(in_sem, inbox.at[pl.ds(0, 6)])
    for h in range(2):
        for o in (1, 2, 3):
            total = total + inbox[h * 4 + o].astype(F32)
    out(total)
    drain(send_sem, src.at[pl.ds(0, 31)])


def ag_wide_part(place, sems, axes, held, use):
    first, second = axes
    f, s = getattr(place, first), getattr(place, second)
    zs = (place.zl, 1 - place.zl)
    steps = (1, 3)
    send_sem, in_sem, pass_sem, near_sem, end_sem = sems

    def block(step, h, o):
        return held.at[((f + step) % 4) * 8 + zs[h] * 4 + (s + o) % 4]

    def ring(h, o):
        for d, step in enumerate(steps):
            sem = pass_sem.at[h * 4 + o] if d == h else near_sem
            push(block(0, h, o), block(0, h, o), send_sem, sem, place.along(first, step))

    def line(h):
        for o in (1, 3, 2):
            push(block(0, h, 0), block(0, h, 0), send_sem, in_sem.at[h * 4 + 4 - o], place.shifted(second, o, 0))

    def arrive(h, o):
        drain(in_sem.at[h * 4 + o], block(0, h, o))
        ring(h, o)

    def pass_on(h, o):
        drain(pass_sem.at[h * 4 + o], block(0, h, o))
        got = block(4 - steps[h], h, o)
        push(got, got, send_sem, end_sem, place.along(first, steps[h]))

    push(block(0, 0, 0), block(0, 0, 0), send_sem, in_sem.at[4], place.shifted(second, 0, 1))
    line(0)
    ring(0, 0)
    yield
    drain(in_sem.at[4], block(0, 1, 0))
    line(1)
    ring(1, 0)
    yield
    arrive(0, 1)
    arrive(0, 3)
    yield
    pass_on(0, 0)
    arrive(0, 2)
    yield
    pass_on(1, 0)
    arrive(1, 1)
    arrive(1, 3)
    yield
    arrive(1, 2)
    pass_on(0, 1)
    pass_on(0, 3)
    yield
    use(f)
    yield
    for h, o in ((0, 2), (1, 1), (1, 3), (1, 2)):
        pass_on(h, o)
    yield
    drain(near_sem, held.at[pl.ds(0, 8)])
    use((f + 1) % 4)
    yield
    use((f + 3) % 4)
    yield
    drain(end_sem, held.at[pl.ds(0, 8)])
    use((f + 2) % 4)
    drain(send_sem, held.at[pl.ds(0, 31)])


def interleave(*parts):
    parts = list(parts)
    while parts:
        left = []
        for part in parts:
            try:
                next(part)
                left.append(part)
            except StopIteration:
                pass
        parts = left


def rs_narrow(place, sems, src, fill, core_recv, temp, z_recv):
    zh, c = place.zh, place.c
    mate, across = place.narrow(0, 1), place.narrow(1, 0)
    parts = [pl.ds(p * 4, 4) for p in range(2)]
    send_sem, near_sem = sems.sender(), sems.receiver()
    far_sems = [sems.receiver() for p in parts]
    cross_sems = [sems.receiver() for p in parts]
    over = (1 - zh) * 2 + 1 - c
    fill(over)
    for p, far_sem in zip(parts, far_sems):
        push(src.at[over, p], core_recv.at[0, p], send_sem, far_sem, mate)
    over = (1 - zh) * 2 + c
    fill(over)
    for p, far_sem, cross_sem in zip(parts, far_sems, cross_sems):
        drain(far_sem, temp.at[p])
        temp[p] = total_of(src[over, p], core_recv[0, p]).astype(BF16)
        push(temp.at[p], z_recv.at[p], send_sem, cross_sem, across)
    fill(zh * 2 + 1 - c)
    push(src.at[zh * 2 + 1 - c], core_recv.at[1], send_sem, near_sem, mate)
    fill(zh * 2 + c)
    drain(near_sem, z_recv)
    for p, cross_sem in zip(parts, cross_sems):
        drain(cross_sem, z_recv.at[p])
    drain(send_sem, src.at[pl.ds(0, 3)])
    return [src.at[zh * 2 + c], core_recv.at[1], z_recv]


def share_scales(place, sems, sums, got, scales):
    send_sem, recv_sem = sems.sender(), sems.receiver()
    for k, (dzh, dc) in enumerate(((0, 1), (1, 0), (1, 1))):
        push(sums, got.at[k], send_sem, recv_sem, place.narrow(dzh, dc))

    def finish():
        drain(recv_sem, got)
        drain(send_sem, got)
        total = sums[...] + got[0] + got[1] + got[2]
        scales[...] = lax.rsqrt(total / D + EPS)

    return finish


def kernel(
    tok_ref,
    len_ref,
    hyena_gain_ref,
    attn_gain_ref,
    taps_ref,
    poles_ref,
    residues_ref,
    skip_ref,
    fir_hbm,
    emb_hbm,
    hyena_in_hbm,
    modal_hbm,
    hyena_out_hbm,
    attn_in_hbm,
    attn_out_hbm,
    kv_hbm,
    out_ref,
    modal_out_hbm,
    fir_out_hbm,
    emb,
    hyena_in,
    modal,
    hyena_out,
    attn_in,
    attn_out,
    kv_raw,
    fir_raw,
    load_sem,
    send_sem,
    recv_sem,
    rs_sem,
    ag_sem,
    tokens,
    xg,
    table,
    zsend,
    zcore,
    ztemp,
    zrecv,
    sums,
    sums_got,
    scales,
    mixers,
    psend,
    far,
    close,
    temp,
    mid,
    inbox,
    over,
    hidden0,
    hidden1,
    held,
    qkv,
    wide_qkv,
    qkv16,
    route_pick,
    att_pick,
    rsend,
    rcore,
    spread16,
    routed,
    turned16,
    scored,
    weights16,
    att_send,
    att_recv,
    att_rows,
    att_full,
):
    place = Place()
    sems = Sems(send_sem, recv_sem)
    w, n = place.w, place.n

    barrier = pltpu.get_barrier_semaphore()

    def peer(d):
        return ((w + d) % 32, ((place.zh + d // 32) % 2) * 2 + place.c)

    def greet(d, carry):
        pl.semaphore_signal(barrier, inc=1, device_id=peer(d), device_id_type=MESH)
        return carry

    lax.fori_loop(1, 32, greet, 0)
    for dzh, dc in ((0, 1), (1, 0), (1, 1)):
        pl.semaphore_signal(barrier, inc=1, device_id=place.narrow(dzh, dc), device_id_type=MESH)

    loads = []
    for k, (src, dst) in enumerate(
        (
            (emb_hbm, emb),
            (hyena_in_hbm, hyena_in),
            (modal_hbm, modal),
            (hyena_out_hbm, hyena_out),
            (attn_in_hbm, attn_in),
            (attn_out_hbm, attn_out),
        )
    ):
        copy = pltpu.make_async_copy(src, dst, load_sem.at[k])
        loads.append(copy)
    loads[0].start()
    loads[1].start()
    loads[2].start()
    fir = fir_raw.reshape(6, 128, 128)
    for c in range(3):
        for half in range(2):
            pltpu.make_async_copy(
                fir_hbm.at[:, c, :, pl.ds(half * 128, 128)], fir_raw.at[c * 2 + half], load_sem.at[8]
            ).start()
    loads[3].start()

    sub8 = lax.broadcasted_iota(jnp.int32, (8, 128), 0)
    lane8 = lax.broadcasted_iota(jnp.int32, (8, 128), 1)
    tile = jnp.zeros((8, 128), jnp.int32)
    for t in range(STEPS):
        for i in range(8):
            tile = jnp.where((sub8 == i) & (lane8 // 64 == t), tok_ref[t, i], tile)
    tokens[w] = tile
    token_send, token_recv = sems.sender(), sems.receiver()

    def token_start(d, carry):
        push(tokens.at[w], tokens.at[w], token_send, token_recv, peer(d))
        return carry

    pl.semaphore_wait(barrier, 34)
    lax.fori_loop(1, 32, token_start, 0)

    lane16 = lax.broadcasted_iota(jnp.int32, (16, 128), 1)
    sub16 = lax.broadcasted_iota(jnp.int32, (16, 128), 0)
    loads[0].wait()

    def gain_rows(k, squares):
        rows = pl.ds(pl.multiple_of(k * 16, 16), 16)
        values = emb[rows, :].astype(F32)
        xg[rows, :] = (values * hyena_gain_ref[...]).astype(BF16)
        return jnp.where(lane16 == k, jnp.sum(values * values, axis=1, keepdims=True), squares)

    sums[0] = lax.fori_loop(0, 32, gain_rows, jnp.zeros((16, 128), F32), unroll=4)
    scales_ready = share_scales(place, sems, sums.at[0], sums_got.at[0], scales.at[0])

    def load_kv(h, carry):
        for j in range(2):
            lanes = pl.ds(pl.multiple_of(h * 128, 128), 128)
            pltpu.make_async_copy(kv_hbm.at[j, :, :, lanes], kv_raw.at[h, j], load_sem.at[6]).start()
        return carry

    loads[1].wait()

    def project(k, carry):
        c, m = k // 2, k % 2
        rows = pl.ds(pl.multiple_of(m * 256, 256), 256)
        table[c, rows, :] = dot(xg[rows, :], hyena_in[c]).astype(BF16)
        return carry

    lax.fori_loop(0, 6, project, 0)
    loads[4].start()
    loads[5].start()
    lax.fori_loop(0, 64, load_kv, 0)

    drain(token_recv, tokens.at[pl.ds(0, 31)])
    drain(token_send, tokens.at[pl.ds(0, 31)])
    vocab = lax.broadcasted_iota(jnp.int32, (128, 512), 1)

    def pick(m):
        rows = tokens[pl.ds(m * 8, 8)].reshape(64, 128)
        column = jnp.concatenate([rows[:, 0:1], rows[:, 64:65]], axis=0)
        hot = (column == vocab).astype(F32).astype(BF16)
        for c in range(3):
            picked = dot(hot, table[c]).astype(BF16).reshape(8, 16, 256)
            zsend[m, :, :, c * 256 : (c + 1) * 256] = picked

    terms = rs_narrow(place, sems, zsend, pick, zcore, ztemp, zrecv)
    scales_ready()

    own = tokens[w]
    mine = jnp.concatenate([own[:, 0:1], own[:, 64:65]], axis=0)
    hot16 = (mine == lax.broadcasted_iota(jnp.int32, (16, 512), 1)).astype(F32).astype(BF16)
    hidden0[...] = dot(hot16, emb[...])

    loads[2].wait()
    pltpu.make_async_copy(fir_raw, fir_raw, load_sem.at[8]).wait()
    poles = poles_ref[...][None]
    residues = residues_ref[...][None]

    def filters(g, carry):
        rows = pl.ds(pl.multiple_of(g * 8, 8), 8)
        own_tokens = tokens[n * 8 + g]
        proj = []
        for t in range(STEPS):
            column = own_tokens[:, t * 64 : t * 64 + 1]
            picked = jnp.zeros((8, 128), F32)
            for r in range(16):
                picked = jnp.where(column == lane8 * 16 + r, scales[0, r : r + 1, :], picked)
            scale = jnp.sum(picked, axis=1, keepdims=True)
            got = qkv[pl.ds(pl.multiple_of(t * 64 + g * 8, 8), 8), :] * scale
            proj.append([got[:, c * 256 : (c + 1) * 256] for c in range(3)])
        olds = []
        for slot in range(2):
            old = []
            for c in range(3):
                halves = [fir[c * 2 + half, pl.ds(g * 16 + slot, 8, stride=2), :] for half in range(2)]
                old.append(jnp.concatenate(halves, axis=1))
            olds.append(old)
        taps = [[taps_ref[k, c : c + 1, :] for c in range(3)] for k in range(3)]
        step0 = [taps[0][c] * proj[0][c] + taps[1][c] * olds[0][c] + taps[2][c] * olds[1][c] for c in range(3)]
        step1 = [taps[0][c] * proj[1][c] + taps[1][c] * proj[0][c] + taps[2][c] * olds[0][c] for c in range(3)]
        for slot in range(2):
            for c in range(3):
                for half in range(2):
                    fir[c * 2 + half, pl.ds(g * 16 + slot, 8, stride=2), :] = proj[1 - slot][c][
                        :, half * 128 : half * 128 + 128
                    ]
        state = modal[rows]
        mixer = []
        for step in (step0, step1):
            gated = step[1] * step[2]
            state = poles * state + gated[:, None, :]
            mixed = jnp.sum(residues * state, axis=1) + skip_ref[...] * gated
            mixer.append(step[0] * mixed)
        modal[rows] = state
        mixers[n, g] = jnp.concatenate(mixer, axis=0).astype(BF16)
        return carry

    def sum_terms(k, carry):
        qkv[pl.ds(pl.multiple_of(k * 16, 16), 16), :] = total_of(terms[0][k], terms[1][k], terms[2][k])
        return carry

    lax.fori_loop(0, 8, sum_terms, 0)
    mixer_send, mixer_recv = sems.sender(), sems.receiver()
    for part in range(2):
        lax.fori_loop(part * 4, part * 4 + 4, filters, 0, unroll=4)
        done = mixers.at[n, pl.ds(part * 4, 4)]
        for dzh, dc in ((1, 0), (1, 1), (0, 1)):
            push(done, done, mixer_send, mixer_recv, place.narrow(dzh, dc))
    modal_store = pltpu.make_async_copy(modal, modal_out_hbm, load_sem.at[7])
    modal_store.start()
    for c in range(3):
        for half in range(2):
            pltpu.make_async_copy(
                fir_raw.at[c * 2 + half], fir_out_hbm.at[:, c, :, pl.ds(half * 128, 128)], load_sem.at[8]
            ).start()

    to_row = lax.broadcasted_iota(jnp.int32, (128, 384), 0)
    from_row = lax.broadcasted_iota(jnp.int32, (128, 384), 1)
    place_in = to_row % 8
    branch = jnp.where(place_in < 2, 0, jnp.where(place_in < 4, 3, 1 + place_in % 2))
    when = jnp.where(place_in < 2, place_in, (place_in - 4) // 2)
    seen = (to_row // 16 == (from_row % 128) // 16) & (branch == from_row // 128)
    for m in range(4):
        hit = seen & (from_row % 16 == when * 8 + m * 2 + (to_row % 16) // 8)
        route_pick[m] = jnp.where(hit, 1.0, 0.0).astype(BF16)
    to_row = lax.broadcasted_iota(jnp.int32, (128, 256), 0)
    from_row = lax.broadcasted_iota(jnp.int32, (128, 256), 1)
    row = (from_row % 2) * 8 + (from_row // 64) * 2 + (from_row % 4) // 2
    for hh in range(2):
        hit = (to_row // 16 == (from_row % 64) // 8) & ((from_row % 8) // 4 == hh) & (to_row % 16 == row)
        att_pick[hh] = jnp.where(hit, 1.0, 0.0).astype(BF16)
    drain(mixer_recv, mixers.at[pl.ds(0, 3)])
    drain(mixer_send, mixers.at[pl.ds(0, 3)])

    def out_projection(k, rows, weights, sink):
        def fill_a(y):
            block = rows[pl.ds(y * 8, 8)].reshape(128, 256)
            psend[k, 0, pl.ds(y * 8, 8)] = dot(block, weights[:, :HALF]).astype(BF16).reshape(8, 16, HALF)

        def fill_b(x):
            block = jnp.concatenate(
                [rows[(y * 2 + zl) * 4 + x] for zl in range(2) for y in range(4)], axis=0
            )
            psend[k, 1, pl.ds(x * 8, 8)] = dot(block, weights[:, HALF:]).astype(BF16).reshape(8, 16, HALF)

        gens = []
        for p, (axes, fill) in enumerate(((("y", "x"), fill_a), (("x", "y"), fill_b))):
            bufs = [b.at[k, p] for b in (far, close, temp, mid, inbox, over)]
            sem = rs_sem.at[k, p]
            rs_sems = (sems.sender(), sem.at[pl.ds(0, 4)], sem.at[pl.ds(4, 4)], sem.at[8], sem.at[pl.ds(9, 4)])
            gens.append(rs_wide_part(place, rs_sems, axes, psend.at[k, p], bufs, fill, sink(p)))
        interleave(*gens)

    loads[3].wait()
    zl, x, y = place.zl, place.x, place.y

    def sink_hidden(p):
        def sink(total):
            cols = pl.ds(p * HALF, HALF)
            hidden1[p] = (hidden0[:, cols] + total).astype(BF16)

        return sink

    out_projection(0, mixers.reshape(32, 16, 256), hyena_out, sink_hidden)
    held[0, (y * 2 + zl) * 4 + x] = hidden1[0]
    held[1, (x * 2 + zl) * 4 + y] = hidden1[1]
    squares = jnp.sum(total_of(hidden1[0]) ** 2 + total_of(hidden1[1]) ** 2, axis=1, keepdims=True)
    sums[1] = jnp.broadcast_to(squares, (16, 128))
    scales_ready = share_scales(place, sems, sums.at[1], sums_got.at[1], scales.at[1])
    loads[4].wait()

    def use_plane(p, plane):
        gain = attn_gain_ref[:, p * HALF : (p + 1) * HALF]
        rows = held[p, pl.ds(plane * 8, 8)].reshape(128, HALF).astype(F32) * gain
        rows = rows.astype(BF16)
        for c in range(3):
            got = dot(rows, attn_in[c, p * HALF : (p + 1) * HALF, :])
            if p == 0:
                wide_qkv[0, c, pl.ds(pl.multiple_of(plane * 128, 128), 128), :] = got
            else:
                for k in range(8):
                    at = pl.multiple_of(((k % 4) * 8 + (k // 4) * 4 + plane) * 16, 16)
                    wide_qkv[1, c, pl.ds(at, 16), :] = got[k * 16 : k * 16 + 16]

    gens = []
    for p, axes in enumerate((("y", "x"), ("x", "y"))):
        sem = ag_sem.at[p]
        ag_sems = (sems.sender(), sem.at[pl.ds(0, 8)], sem.at[pl.ds(8, 8)], sem.at[16], sem.at[17])
        gens.append(ag_wide_part(place, ag_sems, axes, held.at[p], functools.partial(use_plane, p)))
    interleave(*gens)

    def join(k, carry):
        rows = pl.ds(pl.multiple_of(k * 32, 32), 32)
        for c in range(3):
            both = wide_qkv[0, c, rows, :] + wide_qkv[1, c, rows, :]
            qkv16[k // 4, pl.ds(pl.multiple_of(c * 128 + (k % 4) * 32, 32), 32), :] = both.astype(BF16)
        return carry

    lax.fori_loop(0, 16, join, 0, unroll=2)

    def split(m):
        for g in range(4):
            got = dot(route_pick[m], qkv16[g])
            rsend[m, g * 8 : g * 8 + 8] = got.astype(BF16).reshape(8, 16, 256)

    zh, core = place.zh, place.c
    mate = place.narrow(0, 1)
    core_send = sems.sender()
    core_recv = [sems.receiver(), sems.receiver()]
    route_send, route_recv = sems.sender(), sems.receiver()
    for d in (1, 0):
        half = (zh + d) % 2
        split(half * 2 + 1 - core)
        push(rsend.at[half * 2 + 1 - core], rcore.at[half], core_send, core_recv[d], mate)
    split((1 - zh) * 2 + core)
    for d in (1, 0):
        across = (zh + d) % 2
        drain(core_recv[d], rcore.at[0])

        def pack(k, carry):
            spread16[d, k] = total_of(rsend[across * 2 + core, k], rcore[across, k]).astype(BF16)
            return carry

        lax.fori_loop(0, 32, pack, 0, unroll=8)

        def route(k, carry):
            push(
                spread16.at[d, (w + k) % 32],
                routed.at[zh, w],
                route_send,
                route_recv,
                ((w + k) % 32, across * 2 + core),
            )
            return carry

        lax.fori_loop(1 - d, 32, route, 0)
        if d:
            split(zh * 2 + core)
    routed[zh, w] = spread16[0, w]

    kind = sub16 % 8
    late = (kind == 1) | (kind == 6)
    turns = (kind == 0) | (kind == 1) | (kind == 4) | (kind == 6)
    length = jnp.where(sub16 < 8, len_ref[0], len_ref[1])
    place_of = jnp.where(turns, length + jnp.where(late, 1, 0), 0).astype(F32)
    freqs = jnp.exp(-math.log(10000.0) * (lane16 % 64).astype(F32) * 2.0 / HEAD_DIM)
    angles = place_of * freqs
    cos = jnp.cos(angles)
    sin = jnp.where(lane16 < 64, -jnp.sin(angles), jnp.sin(angles))
    lane2 = lax.broadcasted_iota(jnp.int32, (16, 256), 1)
    sub2 = lax.broadcasted_iota(jnp.int32, (16, 256), 0)
    position = (lane2 % 128) // 2
    length2 = jnp.where(sub2 < 8, len_ref[0], len_ref[1])
    valid = (
        (lane2 % 2 == 0)
        & (lane2 // 128 == sub2 // 8)
        & ((position < length2) | (position == 62) | ((position == 63) & (sub2 % 8 == 1)))
    )
    inv = 1.0 / math.sqrt(HEAD_DIM)

    pltpu.make_async_copy(kv_raw, kv_raw, load_sem.at[6]).wait()
    kv = kv_raw.reshape(64, 256, 128)
    routed_all = routed.reshape(64, 16, 256)
    scales_ready()
    row_scale = jnp.zeros((16, 128), F32)
    for t in range(2):
        for j in range(2):
            here = scales[1, pl.ds(t * 8 + n * 2 + j, 1), :]
            own_rows = (sub16 == j * 8 + t) | (sub16 == j * 8 + 4 + 2 * t) | (sub16 == j * 8 + 5 + 2 * t)
            row_scale = jnp.where(own_rows, here, row_scale)
    drain(route_recv, routed_all.at[pl.ds(0, 63)])
    drain(route_send, routed_all.at[pl.ds(0, 63)])
    drain(core_send, rcore)

    def turn(k, carry):
        for hh in range(2):
            h = k * 2 + hh
            lanes = slice(hh * 128, hh * 128 + 128)
            vectors = total_of(routed[0, k, :, lanes], routed[1, k, :, lanes]) * row_scale
            vectors = vectors.astype(BF16).astype(F32)
            turned = vectors * cos + pltpu.roll(vectors, 64, axis=1) * sin
            turned16[h] = turned.astype(BF16)
            for j in range(2):
                old = kv[h, j * 128 + 112 : j * 128 + 128, :].astype(F32)
                fresh = jnp.where(sub8 >= 4, turned[j * 8 : j * 8 + 8], old[8:16])
                kv[h, j * 128 + 112 : j * 128 + 128, :] = jnp.concatenate([old[0:8], fresh], axis=0).astype(BF16)
        return carry

    lax.fori_loop(0, 32, turn, 0, unroll=4)

    def score(h, carry):
        scored[h] = dot_t(turned16[h], kv[h])
        return carry

    lax.fori_loop(0, 64, score, 0, unroll=8)

    def soften(h, carry):
        score = jnp.where(valid, scored[h] * inv, -1e30)
        grown = jnp.exp(score - jnp.max(score, axis=1, keepdims=True))
        weight = grown * (1.0 / jnp.sum(grown, axis=1, keepdims=True))
        weights16[h] = pltpu.roll(weight, 1, axis=1).astype(BF16)
        return carry

    lax.fori_loop(0, 64, soften, 0, unroll=8)

    att_out_sem, att_in_sem = sems.sender(), sems.receiver()

    def attend(i, carry):
        tiles = [(w + i * 4 + u) % 32 for u in range(4)]
        for k in tiles:
            message = jnp.zeros((8, 128), F32)
            for hh in range(2):
                got = dot(weights16[k * 2 + hh], kv[k * 2 + hh])
                for j in range(2):
                    at = hh * 4 + j * 2
                    moved = pltpu.roll(got[j * 8 : j * 8 + 8], at, axis=0) if at else got[0:8]
                    message = jnp.where((sub8 >= at) & (sub8 < at + 2), moved, message)
            att_send[k] = message.astype(BF16).astype(F32)
        for k in tiles:
            push(att_send.at[k], att_recv.at[zh, w], att_out_sem, att_in_sem, (k, (1 - zh) * 2 + core))
        return carry

    lax.fori_loop(0, 8, attend, 0)

    def spread_att(d, carry):
        push(att_send.at[(w + d) % 32], att_recv.at[zh, w], att_out_sem, att_in_sem, peer(d))
        return carry

    lax.fori_loop(1, 32, spread_att, 0)
    att_recv[zh, w] = att_send[w]
    att_all = att_recv.reshape(64, 8, 128)
    drain(att_in_sem, att_all.at[pl.ds(0, 63)])
    swap_send, swap_recv = sems.sender(), sems.receiver()
    for m in range(2):

        def take(k, carry):
            pair = att_recv[m, pl.ds(k * 2, 2)].reshape(16, 128)
            att_rows[m * 2 + core, k] = pair.astype(BF16)
            return carry

        lax.fori_loop(0, 16, take, 0, unroll=8)
        block = att_rows.at[m * 2 + core]
        push(block, block, swap_send, swap_recv, mate)
    drain(swap_recv, att_rows.at[pl.ds(0, 2)])
    drain(swap_send, att_rows.at[pl.ds(0, 2)])
    drain(att_out_sem, att_all.at[pl.ds(0, 63)])
    for g in range(4):
        stack = jnp.concatenate([att_rows[m, g * 4 : g * 4 + 4].reshape(64, 128) for m in range(4)], axis=0)
        got = jnp.concatenate([dot(att_pick[hh], stack) for hh in range(2)], axis=1)
        att_full[g * 8 : g * 8 + 8] = got.astype(BF16).reshape(8, 16, 256)
    loads[5].wait()

    def sink_out(p):
        def sink(total):
            cols = pl.ds(p * HALF, HALF)
            rows = (hidden1[p].astype(F32) + total).astype(BF16)
            out_ref[0, :, cols] = rows[0:8]
            out_ref[1, :, cols] = rows[8:16]

        return sink

    out_projection(1, att_full, attn_out, sink_out)
    modal_store.wait()
    pltpu.make_async_copy(fir_raw, fir_raw, load_sem.at[8]).wait()


def hand_over(a, b, c, out_a, out_b, out_c, held_a, held_b, held_c, sem):
    steps = ((a, held_a, out_a), (b, held_b, out_b), (c, held_c, out_c))
    ins = [pltpu.make_async_copy(src, held, sem.at[k]) for k, (src, held, _) in enumerate(steps)]
    outs = [pltpu.make_async_copy(held, dst, sem.at[3 + k]) for k, (_, held, dst) in enumerate(steps)]
    for copy in ins:
        copy.start()
    for copy_in, copy_out in zip(ins, outs):
        copy_in.wait()
        copy_out.start()
    for copy in outs:
        copy.wait()


def local(
    token_ids,
    lengths,
    embedding,
    hyena_gain,
    hyena_in,
    fir_taps,
    poles,
    residues,
    skip,
    hyena_out,
    modal_state,
    fir_state,
    attn_gain,
    attn_in,
    attn_out,
    kv_cache,
):
    vmem = pl.BlockSpec(memory_space=pltpu.VMEM)
    smem = pl.BlockSpec(memory_space=pltpu.SMEM)
    anywhere = pl.BlockSpec(memory_space=pl.ANY)
    out, modal_out, fir_out = pl.pallas_call(
        kernel,
        out_shape=(
            jax.ShapeDtypeStruct((2, 8, 2048), BF16),
            jax.ShapeDtypeStruct((64, 16, 256), F32),
            jax.ShapeDtypeStruct((64, 3, 2, 256), F32),
        ),
        in_specs=[smem] * 2 + [vmem] * 6 + [anywhere] * 8,
        out_specs=(vmem, anywhere, anywhere),
        scratch_shapes=[
            pltpu.VMEM((512, 2048), BF16),
            pltpu.VMEM((3, 2048, 256), BF16),
            pltpu.VMEM((64, 16, 256), F32),
            pltpu.VMEM((256, 2048), BF16),
            pltpu.VMEM((3, 2048, 256), BF16),
            pltpu.VMEM((256, 2048), BF16),
            pltpu.VMEM((64, 2, 64, 2, 128), BF16),
            pltpu.VMEM((6, 64, 2, 128), F32),
            pltpu.SemaphoreType.DMA((9,)),
            pltpu.SemaphoreType.DMA((16,)),
            pltpu.SemaphoreType.DMA((22,)),
            pltpu.SemaphoreType.DMA((2, 2, 13)),
            pltpu.SemaphoreType.DMA((2, 18)),
            pltpu.VMEM((32, 8, 128), jnp.int32),
            pltpu.VMEM((512, 2048), BF16),
            pltpu.VMEM((3, 512, 256), BF16),
            pltpu.VMEM((4, 8, 16, 768), BF16),
            pltpu.VMEM((2, 8, 16, 768), BF16),
            pltpu.VMEM((8, 16, 768), BF16),
            pltpu.VMEM((8, 16, 768), BF16),
            pltpu.VMEM((2, 16, 128), F32),
            pltpu.VMEM((2, 3, 16, 128), F32),
            pltpu.VMEM((2, 16, 128), F32),
            pltpu.VMEM((4, 8, 16, 256), BF16),
            pltpu.VMEM((2, 2, 32, 16, HALF), BF16),
            pltpu.VMEM((2, 2, 4, 2, 16, HALF), BF16),
            pltpu.VMEM((2, 2, 4, 4, 16, HALF), BF16),
            pltpu.VMEM((2, 2, 4, 2, 16, HALF), BF16),
            pltpu.VMEM((2, 2, 8, 16, HALF), BF16),
            pltpu.VMEM((2, 2, 8, 16, HALF), BF16),
            pltpu.VMEM((2, 2, 4, 16, HALF), BF16),
            pltpu.VMEM((16, 2048), F32),
            pltpu.VMEM((2, 16, HALF), BF16),
            pltpu.VMEM((2, 32, 16, HALF), BF16),
            pltpu.VMEM((128, 768), F32),
            pltpu.VMEM((2, 3, 512, 256), F32),
            pltpu.VMEM((4, 384, 256), BF16),
            pltpu.VMEM((4, 128, 384), BF16),
            pltpu.VMEM((2, 128, 256), BF16),
            pltpu.VMEM((4, 32, 16, 256), BF16),
            pltpu.VMEM((2, 32, 16, 256), BF16),
            pltpu.VMEM((2, 32, 16, 256), BF16),
            pltpu.VMEM((2, 32, 16, 256), BF16),
            pltpu.VMEM((64, 16, 128), BF16),
            pltpu.VMEM((64, 16, 256), F32),
            pltpu.VMEM((64, 16, 256), BF16),
            pltpu.VMEM((32, 8, 128), F32),
            pltpu.VMEM((2, 32, 8, 128), F32),
            pltpu.VMEM((4, 16, 16, 128), BF16),
            pltpu.VMEM((32, 16, 256), BF16),
        ],
        compiler_params=pltpu.CompilerParams(
            collective_id=0, has_side_effects=True, vmem_limit_bytes=56 * 1024 * 1024
        ),
        name="decode",
    )(
        token_ids,
        lengths,
        hyena_gain[None, :],
        attn_gain[None, :],
        fir_taps,
        poles,
        residues,
        skip[None, :],
        fir_state.transpose(0, 2, 1, 3),
        embedding,
        hyena_in.transpose(1, 0, 2),
        modal_state,
        hyena_out,
        attn_in.transpose(1, 0, 2),
        attn_out,
        kv_cache,
    )
    made = (out, modal_out, fir_out)
    out, modal_out, fir_out = pl.pallas_call(
        hand_over,
        out_shape=[jax.ShapeDtypeStruct(array.shape, array.dtype) for array in made],
        in_specs=[anywhere] * 3,
        out_specs=[anywhere] * 3,
        scratch_shapes=[pltpu.VMEM(array.shape, array.dtype) for array in made]
        + [pltpu.SemaphoreType.DMA((6,))],
        name="hand_over",
    )(*made)
    return out, modal_out, fir_out.transpose(0, 2, 1, 3)


def solution(mesh):
    placed = (
        P(None, "wide"),
        P(("wide", "narrow")),
        P(None, "narrow"),
        P("narrow"),
        P("narrow", None, "wide"),
        P(None, None, "wide"),
        P(None, "wide"),
        P(None, "wide"),
        P("wide"),
        P("wide", "narrow"),
        P("narrow", None, "wide"),
        P("narrow", None, None, "wide"),
        P("narrow"),
        P("narrow", None, "wide"),
        P("wide", "narrow"),
        P(("wide", "narrow"), None, None, None),
    )
    return jax.shard_map(
        local,
        mesh=mesh,
        in_specs=placed,
        out_specs=(
            P(None, "wide", "narrow"),
            P("narrow", None, "wide"),
            P("narrow", None, None, "wide"),
        ),
        check_vma=False,
    )
```
